128 devices in a mesh: ray: 16 (over x, y), brick: 8 (over z, core).
Axes of the slice: x: 4, y: 4, z: 4, core: 2. Of those that a mesh axis runs over, the one named last changes fastest.
Arguments:
- estimate: float32 [4, 8192, 128], P(None, ('ray', 'brick')), may hold values from -6 to 6
- blocks: bfloat16 [8, 256, 128, 4096], P('brick', 'ray'), may hold values from -0.0625 to 0.0625
- block_bundle: int32 [8, 256], P('brick', 'ray'), may hold values from 0 to 127
- sinogram: float32 [8, 128, 4, 128], P('brick', 'ray'), may hold values from -6 to 6
Outputs:
- restored: float32 [4, 8192, 128], P(None, ('ray', 'brick'))
- residual: float32 [8, 128, 4, 128], P('brick', 'ray')
The draws below stay inside these ranges and needn't reach their ends.
All inputs are finite; a program needn't handle non-finite values.
Results may differ from the reference program's by a relative error of at most 0.0031.
Values may be sent and summed in bfloat16 or wider, within the bound.
A program may use at most 64 MiB of HBM per device.

```python
import jax
import jax.numpy as jnp
from jax import lax

SLICES = 4
TSIDE = 64
RAYS = 128
BUNDLES = 128
BCOLS = 2
SWEEPS = 3
ANGLES = 8
TROWS = 128
TILES = 256
HEIGHT = 8192
WIDTH = 128


def set_ends(drawn, key, smallest, high):
    longest = drawn.shape.index(max(drawn.shape))
    spots = []
    for shift in (0, 1):
        where = [jax.random.randint(jax.random.fold_in(key, axis), (), 0, length) for axis, length in enumerate(drawn.shape)]
        where[longest] = (where[longest] + shift) % drawn.shape[longest]
        spots.append(tuple(where))
    return drawn.at[spots[0]].set(smallest).at[spots[1]].set(high)


def steps_of(rng, extent, cuts, least, high):
    def one(dim, blocks):
        heights = jax.random.uniform(jax.random.fold_in(jax.random.fold_in(rng, 6), dim), (blocks,), jnp.float32, least / len(cuts), high / len(cuts))
        return jnp.repeat(jnp.exp(heights), extent[dim] // blocks).reshape((-1,) + (1,) * (len(extent) - dim - 1))

    gain = one(*cuts[0])
    for cut in cuts[1:]:
        gain = gain * one(*cut)
    return gain


def scatter_about(key, extent, spread, reach, split=(), held_as=jnp.bfloat16):
    entries = spread * jax.random.normal(key, extent, jnp.float32)
    if split:
        entries = entries * steps_of(key, extent, split, -0.22, 0.18)
    return jnp.clip(entries, -reach, reach).astype(held_as)


def setup_inputs(seed: int = 0) -> dict:
    streams_of = jax.random.split(jax.random.key(seed), 5)
    estimate = scatter_about(streams_of[0], (SLICES, HEIGHT, WIDTH), 1.0, 6.0, ((1, 128),), jnp.float32)
    blocks = scatter_about(streams_of[1], (ANGLES, TILES, RAYS, TSIDE * TSIDE), (TSIDE * TSIDE * TILES // BUNDLES) ** -0.5, 0.0625, ((0, 8), (1, 16)))
    block_bundle = set_ends(jax.random.randint(streams_of[2], (ANGLES, TILES), 0, BUNDLES), jax.random.fold_in(streams_of[2], 1), 0, BUNDLES - 1).astype(jnp.int32)
    sinogram = scatter_about(streams_of[3], (ANGLES, BUNDLES, SLICES, RAYS), 1.0, 6.0, ((0, 8), (1, 16)), jnp.float32)
    return dict(estimate=estimate, blocks=blocks, block_bundle=block_bundle, sinogram=sinogram)


step_size = 0.5
tv_step = 0.28
tv_weight = 0.5

def forward_diffs(field):
    diff_y = jnp.concatenate([field[:, 1:, :], jnp.zeros_like(field[:, :1, :])], axis=1) - field
    diff_x = jnp.concatenate([field[:, :, 1:], jnp.zeros_like(field[:, :, :1])], axis=2) - field
    diff_z = jnp.concatenate([field[1:] - field[:-1], jnp.zeros_like(field[:1])], axis=0)
    return (diff_y, diff_x, diff_z)

def divergence_of(dual_y, dual_x, dual_z):
    part_y = dual_y - jnp.concatenate([jnp.zeros_like(dual_y[:, :1, :]), dual_y[:, :-1, :]], axis=1)
    part_x = dual_x - jnp.concatenate([jnp.zeros_like(dual_x[:, :, :1]), dual_x[:, :, :-1]], axis=2)
    part_z = dual_z - jnp.concatenate([jnp.zeros_like(dual_z[:1]), dual_z[:-1]], axis=0)
    return part_y + part_x + part_z

def dual_update(dual_y, dual_x, dual_z, diff_y, diff_x, diff_z):
    trial_y = dual_y + tv_step * diff_y
    trial_x = dual_x + tv_step * diff_x
    trial_z = dual_z + tv_step * diff_z
    shrink = jnp.sqrt(jnp.maximum(1.0, (trial_y * trial_y + trial_x * trial_x + trial_z * trial_z) / (tv_weight * tv_weight)))
    return (trial_y / shrink, trial_x / shrink, trial_z / shrink)

def reference(estimate, blocks, block_bundle, sinogram):
    rounded_image = estimate.astype(jnp.bfloat16)
    rounded_image = lax.optimization_barrier(rounded_image)
    tile_values = rounded_image.astype(jnp.float32).reshape(SLICES, TROWS, TSIDE, BCOLS, TSIDE)
    tile_values = tile_values.transpose(1, 3, 0, 2, 4).reshape(TILES, SLICES, TSIDE * TSIDE)
    labels = jnp.arange(BUNDLES, dtype=jnp.int32)

    def project(pieces):
        block_set, bundle_ids = pieces
        contrib = jnp.einsum('tsp,trp->tsr', tile_values, block_set.astype(jnp.float32), precision=lax.Precision.HIGHEST)
        onehot = (bundle_ids[None, :] == labels[:, None]).astype(jnp.float32)
        return jnp.einsum('bt,tsr->bsr', onehot, contrib, precision=lax.Precision.HIGHEST)
    projected = lax.map(project, (blocks, block_bundle))
    residual = projected - sinogram
    rounded_residual = lax.optimization_barrier(residual.astype(jnp.bfloat16)).astype(jnp.float32)

    def backward(running, pieces):
        block_set, bundle_ids, residual_rows = pieces
        picked = residual_rows[bundle_ids]
        return (running + jnp.einsum('tsr,trp->tsp', picked, block_set.astype(jnp.float32), precision=lax.Precision.HIGHEST), None)
    grad_tiles, _ = lax.scan(backward, jnp.zeros((TILES, SLICES, TSIDE * TSIDE), jnp.float32), (blocks, block_bundle, rounded_residual))
    grad_image = grad_tiles.reshape(TROWS, BCOLS, SLICES, TSIDE, TSIDE).transpose(2, 0, 3, 1, 4).reshape(SLICES, HEIGHT, WIDTH)
    anchor = estimate - step_size * grad_image
    primal = anchor
    extrapolated = anchor
    dual_y = jnp.zeros_like(anchor)
    dual_x = jnp.zeros_like(anchor)
    dual_z = jnp.zeros_like(anchor)
    for sweep in range(SWEEPS):
        diff_y, diff_x, diff_z = forward_diffs(extrapolated)
        dual_y, dual_x, dual_z = dual_update(dual_y, dual_x, dual_z, diff_y, diff_x, diff_z)
        updated = (primal + tv_step * divergence_of(dual_y, dual_x, dual_z) + tv_step * anchor) / (1.0 + tv_step)
        extrapolated = 2.0 * updated - primal
        primal = updated
    return (primal, residual)
```

```python
import jax
import jax.numpy as jnp
from jax import lax
from jax.experimental import pallas as pl
from jax.experimental.pallas import tpu as pltpu
from jax.sharding import PartitionSpec as P

RAY = 16
BRICK = 8
SWEEPS = 3
MESH = pl.DeviceIdType.MESH
BF = jnp.bfloat16
F32 = jnp.float32

step_size = 0.5
tv_step = 0.28
tv_weight = 0.5


def offsets(m):
    g = m // 2
    return g + (g // 2) * (1 - 2 * (g % 2)), m % 2


def kernel(
    est_hbm, blocks_hbm, bundle_ref, sino_hbm,
    out_ref, res_ref,
    est, sino, tiles, tmp, weights, meta, contrib, picked, grad_out, grad_in,
    halo_top, halo_low, est_top, est_low, gathered, anchor,
    load_sem, weight_sem, tile_send, tile_recv, meta_send, meta_recv, con_send, con_recv,
    grad_send, grad_recv, top_send, top_recv, low_send, low_recv, edge_send, edge_recv,
):
    ray = lax.axis_index("ray")
    brick = lax.axis_index("brick")
    z, core = brick // 2, brick % 2

    def forward_peer(m):
        dz, dc = offsets(m)
        return ((z + dz) % 4) * 2 + (core + dc) % 2

    def backward_peer(m):
        dz, dc = offsets(m)
        return ((z + 4 - dz) % 4) * 2 + (core + dc) % 2

    load_est = pltpu.make_async_copy(est_hbm, est, load_sem.at[0])
    load_sino = pltpu.make_async_copy(sino_hbm, sino, load_sem.at[1])
    load_est.start()
    load_sino.start()

    def load_block(m, _):
        pltpu.make_async_copy(
            blocks_hbm.at[0, pl.ds(2 * forward_peer(m), 2)], weights.at[m], weight_sem.at[m]
        ).start()
        return 0

    lax.fori_loop(0, BRICK, load_block, 0)

    barrier = pltpu.get_barrier_semaphore()
    for m in range(1, BRICK):
        pl.semaphore_signal(
            barrier, inc=1, device_id={"ray": ray, "brick": forward_peer(m)}, device_id_type=MESH
        )
    for d in range(1, RAY):
        pl.semaphore_signal(
            barrier, inc=1, device_id={"ray": (ray + d) % RAY, "brick": brick}, device_id_type=MESH
        )

    @pl.when(brick == 0)
    def _():
        for b in range(BRICK):
            pl.semaphore_signal(
                barrier, inc=1, device_id={"ray": (ray + RAY - 1) % RAY, "brick": b}, device_id_type=MESH
            )

    @pl.when(brick == BRICK - 1)
    def _():
        for b in range(BRICK):
            pl.semaphore_signal(
                barrier, inc=1, device_id={"ray": (ray + 1) % RAY, "brick": b}, device_id_type=MESH
            )

    lane = lax.broadcasted_iota(jnp.int32, (8, 128), 1)
    row = lax.broadcasted_iota(jnp.int32, (8, 128), 0)
    lane32 = lax.broadcasted_iota(jnp.int32, (32, 128), 1)

    load_est.wait()
    for s in range(4):
        even = est[s, pl.ds(0, 32, stride=2), :]
        odd = est[s, pl.ds(1, 32, stride=2), :]
        tmp[pl.ds(s, 32, stride=8), :] = jnp.where(lane32 < 64, even, pltpu.roll(odd, 64, 1))
        tmp[pl.ds(4 + s, 32, stride=8), :] = jnp.where(lane32 < 64, pltpu.roll(even, 64, 1), odd)
    tiles[0] = tmp[...].astype(BF).reshape(16, 16, 128)

    row_keys = []
    lane_key = jnp.zeros((8, 128), F32)
    for m in range(BRICK):
        first = bundle_ref[0, 2 * forward_peer(m)].astype(F32)
        second = bundle_ref[0, 2 * forward_peer(m) + 1].astype(F32)
        both = jnp.where(row < 4, first, second)
        row_keys.append(both * 4.0 + (row % 4).astype(F32))
        lane_key = jnp.where((lane % 64) // 8 == m, jnp.where((lane // 4) % 2 == 0, first, second), lane_key)
    load_sino.wait()
    meta[0, 0:32, :] = sino[...].astype(BF)
    meta[0, 32:48, :] = jnp.concatenate([lane_key, lane_key], axis=0).astype(BF)

    pl.semaphore_wait(barrier, BRICK - 1 + RAY - 1 + 2)

    def tile_copy(m):
        return pltpu.make_async_remote_copy(
            src_ref=tiles.at[0], dst_ref=tiles.at[m], send_sem=tile_send.at[m], recv_sem=tile_recv.at[m],
            device_id={"ray": ray, "brick": backward_peer(m)}, device_id_type=MESH,
        )

    def meta_copy(d):
        return pltpu.make_async_remote_copy(
            src_ref=meta.at[0], dst_ref=meta.at[RAY - d], send_sem=meta_send.at[d], recv_sem=meta_recv.at[RAY - d],
            device_id={"ray": (ray + d) % RAY, "brick": brick}, device_id_type=MESH,
        )

    above = (brick + BRICK - 1) % BRICK
    above_ray = (ray + (brick + BRICK - 1) // BRICK + RAY - 1) % RAY
    below = (brick + 1) % BRICK
    below_ray = (ray + (brick + 1) // BRICK) % RAY
    edge_down = pltpu.make_async_remote_copy(
        src_ref=est.at[:, pl.ds(56, 8), :], dst_ref=est_top, send_sem=edge_send.at[0], recv_sem=edge_recv.at[0],
        device_id={"ray": below_ray, "brick": below}, device_id_type=MESH,
    )
    edge_up = pltpu.make_async_remote_copy(
        src_ref=est.at[:, pl.ds(0, 8), :], dst_ref=est_low, send_sem=edge_send.at[1], recv_sem=edge_recv.at[1],
        device_id={"ray": above_ray, "brick": above}, device_id_type=MESH,
    )

    for m in range(1, BRICK):
        tile_copy(m).start()
    for d in range(1, RAY):
        meta_copy(d).start()
    edge_down.start()
    edge_up.start()

    def con_copy(g, d):
        return pltpu.make_async_remote_copy(
            src_ref=contrib.at[0, pl.ds(g * 16, 16)], dst_ref=contrib.at[RAY - d, pl.ds(g * 16, 16)],
            send_sem=con_send.at[g, d], recv_sem=con_recv.at[g, RAY - d],
            device_id={"ray": (ray + d) % RAY, "brick": brick}, device_id_type=MESH,
        )

    def project(m, _):
        pltpu.make_async_copy(weights.at[m], weights.at[m], weight_sem.at[m]).wait()

        @pl.when(m > 0)
        def _():
            tile_copy(m).wait_recv()

        held = tiles[m].astype(F32)
        left = jnp.concatenate(
            [half for c in range(16) for half in (held[c, 0:8], held[c, 8:16])], axis=1
        ).astype(BF)
        full = lax.dot_general(
            left, weights[m].reshape(256, 4096), (((1,), (1,)), ((), ())), preferred_element_type=F32
        )
        picked[pl.ds(pl.multiple_of(m * 8, 8), 8), :] = jnp.where(row < 4, full[:, :128], full[:, 128:])

        @pl.when(m % 2 == 1)
        def _():
            g = m // 2
            at = pl.multiple_of(g * 16, 16)
            contrib[0, pl.ds(at, 16), :] = picked[pl.ds(at, 16), :].astype(BF)
            for d in range(1, RAY):
                con_copy(g, d).start()

        return 0

    lax.fori_loop(0, BRICK, project, 0)

    for d in range(1, RAY):
        meta_copy(d).wait_recv()
    own_first = (ray * 32).astype(F32)
    for b in range(4):
        row_keys.append(own_first + (b * 8 + row).astype(F32))
    row_keys = jnp.concatenate(row_keys, axis=0)
    columns = []
    for q in range(RAY // 2):
        key = jnp.where(
            lane < 64, meta[2 * q, 32:48, :].astype(F32)[0:8], meta[2 * q + 1, 32:48, :].astype(F32)[0:8]
        ) * 4.0 + (lane % 4).astype(F32)
        columns.append(jnp.where(row_keys == jnp.concatenate([key] * 12, axis=0), 1.0, 0.0))
    row_all = lax.broadcasted_iota(jnp.int32, (96, 128), 0)
    for q in range(4):
        owner = (ray + 4 * q + lane // 32) % RAY
        key = (owner * 32 + lane % 32).astype(F32)
        hit = (row_keys == jnp.concatenate([key] * 12, axis=0)) & (row_all < 64)
        columns.append(jnp.where(hit, -1.0, 0.0))
    select = jnp.concatenate(columns, axis=1).astype(BF)
    sinos = meta[:, 0:32, :].reshape(512, 128)

    for g in range(4):
        for d in range(1, RAY):
            con_copy(g, d).wait_recv()
    right = jnp.concatenate([contrib[...].reshape(1024, 128), sinos], axis=0)
    resid = jnp.dot(select, right, preferred_element_type=F32)
    picked[...] = resid[0:64]
    res_ref[...] = resid[64:96] - sino[...]

    def grad_copy(m):
        return pltpu.make_async_remote_copy(
            src_ref=grad_out.at[m], dst_ref=grad_in.at[m], send_sem=grad_send.at[m], recv_sem=grad_recv.at[m],
            device_id={"ray": ray, "brick": forward_peer(m)}, device_id_type=MESH,
        )

    def halo_copies(m):
        tile_row = forward_peer(m)
        down = (tile_row + 1) % BRICK
        down_ray = (ray + (tile_row + 1) // BRICK) % RAY
        up = (tile_row + BRICK - 1) % BRICK
        up_ray = (ray + (tile_row + BRICK - 1) // BRICK + RAY - 1) % RAY
        own_down = (down == brick) & (down_ray == ray)
        own_up = (up == brick) & (up_ray == ray)
        to_down = pltpu.make_async_remote_copy(
            src_ref=grad_out.at[m, 15], dst_ref=halo_top.at[brick], send_sem=top_send.at[m],
            recv_sem=top_recv.at[brick], device_id={"ray": down_ray, "brick": down}, device_id_type=MESH,
        )
        here_down = pltpu.make_async_copy(grad_out.at[m, 15], halo_top.at[brick], top_recv.at[brick])
        to_up = pltpu.make_async_remote_copy(
            src_ref=grad_out.at[m, 0], dst_ref=halo_low.at[brick], send_sem=low_send.at[m],
            recv_sem=low_recv.at[brick], device_id={"ray": up_ray, "brick": up}, device_id_type=MESH,
        )
        here_up = pltpu.make_async_copy(grad_out.at[m, 0], halo_low.at[brick], low_recv.at[brick])
        return own_down, own_up, to_down, here_down, to_up, here_up

    def backproject(step, _):
        m = BRICK - 1 - step
        mine = picked[pl.ds(pl.multiple_of(m * 8, 8), 8), :]
        left = jnp.concatenate(
            [jnp.where(row < 4, mine, 0.0), jnp.where(row < 4, 0.0, mine)], axis=1
        ).astype(BF)
        spread = jnp.dot(left, weights[m].reshape(256, 4096), preferred_element_type=F32)
        for c in range(16):
            grad_out[m, c] = jnp.concatenate(
                [spread[:, c * 256 : c * 256 + 128], spread[:, c * 256 + 128 : c * 256 + 256]], axis=0
            ).astype(BF)

        @pl.when(m > 0)
        def _():
            grad_copy(m).start()

        own_down, own_up, to_down, here_down, to_up, here_up = halo_copies(m)
        pl.when(own_down)(here_down.start)
        pl.when(jnp.logical_not(own_down))(to_down.start)
        pl.when(own_up)(here_up.start)
        pl.when(jnp.logical_not(own_up))(to_up.start)
        return 0

    lax.fori_loop(0, BRICK, backproject, 0)

    edge_down.wait_recv()
    edge_up.wait_recv()
    for b in range(BRICK):
        pltpu.make_async_copy(halo_top.at[b], halo_top.at[b], top_recv.at[b]).wait()
        pltpu.make_async_copy(halo_low.at[b], halo_low.at[b], low_recv.at[b]).wait()
    gathered[0:16, :] = halo_top[...].astype(F32).sum(axis=0)
    gathered[272:288, :] = halo_low[...].astype(F32).sum(axis=0)
    total = grad_out[0].astype(F32)
    for m in range(1, BRICK):
        grad_copy(m).wait_recv()
        total += grad_in[m].astype(F32)
    gathered[16:272, :] = total.reshape(256, 128)

    lane36 = lax.broadcasted_iota(jnp.int32, (36, 128), 1)
    for s in range(4):
        one = gathered[pl.ds(s, 36, stride=8), :]
        two = gathered[pl.ds(4 + s, 36, stride=8), :]
        anchor[s, pl.ds(0, 36, stride=2), :] = jnp.where(lane36 < 64, one, pltpu.roll(two, 64, 1))
        anchor[s, pl.ds(1, 36, stride=2), :] = jnp.where(lane36 < 64, pltpu.roll(one, 64, 1), two)
    image = jnp.concatenate([est_top[:, 4:8, :], est[...], est_low[:, 0:4, :]], axis=1)
    start = image - step_size * anchor[...]

    shape = (4, 72, 128)
    rows = lax.broadcasted_iota(jnp.int32, shape, 1)
    lanes = lax.broadcasted_iota(jnp.int32, shape, 2)
    at_start = (ray == 0) & (brick == 0)
    at_end = (ray == RAY - 1) & (brick == BRICK - 1)
    above_image = (rows < 4) & at_start
    below_image = (rows >= 68) & at_end
    last_lane = lanes == 127
    first_lane = lanes == 0
    level = jnp.zeros((1, 72, 128), F32)

    start = jnp.where(below_image, 0.0, start)
    primal = start
    extra = start
    dual_y = dual_x = dual_z = None
    for sweep in range(SWEEPS):
        diff_y = pltpu.roll(extra, 71, 1) - extra
        diff_x = jnp.where(last_lane, 0.0, pltpu.roll(extra, 127, 2)) - extra
        diff_z = jnp.concatenate([extra[1:] - extra[:-1], level], axis=0)
        trial_y, trial_x, trial_z = tv_step * diff_y, tv_step * diff_x, tv_step * diff_z
        if sweep:
            trial_y, trial_x, trial_z = dual_y + trial_y, dual_x + trial_x, dual_z + trial_z
        norm = trial_y * trial_y + trial_x * trial_x + trial_z * trial_z
        shrink = lax.rsqrt(jnp.maximum(1.0, norm * (1.0 / (tv_weight * tv_weight))))
        dual_y = jnp.where(above_image, 0.0, trial_y * shrink)
        dual_x = trial_x * shrink
        dual_z = trial_z * shrink
        div = dual_y - pltpu.roll(dual_y, 1, 1)
        div += dual_x - jnp.where(first_lane, 0.0, pltpu.roll(dual_x, 1, 2))
        div += dual_z - jnp.concatenate([level, dual_z[:-1]], axis=0)
        updated = (primal + tv_step * div + tv_step * start) * (1.0 / (1.0 + tv_step))
        extra = jnp.where(below_image, 0.0, 2.0 * updated - primal)
        primal = updated
    out_ref[...] = primal[:, 4:68, :]

    for m in range(1, BRICK):
        tile_copy(m).wait_send()
        grad_copy(m).wait_send()
    for d in range(1, RAY):
        meta_copy(d).wait_send()
        for g in range(4):
            con_copy(g, d).wait_send()
    edge_down.wait_send()
    edge_up.wait_send()
    for m in range(BRICK):
        own_down, own_up, to_down, here_down, to_up, here_up = halo_copies(m)
        pl.when(jnp.logical_not(own_down))(to_down.wait_send)
        pl.when(jnp.logical_not(own_up))(to_up.wait_send)


def shards(estimate, blocks, block_bundle, sinogram):
    dma = pltpu.SemaphoreType.DMA
    restored, residual = pl.pallas_call(
        kernel,
        out_shape=(
            jax.ShapeDtypeStruct((4, 64, 128), F32),
            jax.ShapeDtypeStruct((32, 128), F32),
        ),
        in_specs=[
            pl.BlockSpec(memory_space=pl.ANY),
            pl.BlockSpec(memory_space=pl.ANY),
            pl.BlockSpec(memory_space=pltpu.SMEM),
            pl.BlockSpec(memory_space=pl.ANY),
        ],
        out_specs=(pl.BlockSpec(memory_space=pltpu.VMEM), pl.BlockSpec(memory_space=pltpu.VMEM)),
        scratch_shapes=[
            pltpu.VMEM((4, 64, 128), F32),
            pltpu.VMEM((32, 128), F32),
            pltpu.VMEM((BRICK, 16, 16, 128), BF),
            pltpu.VMEM((256, 128), F32),
            pltpu.VMEM((BRICK, 2, 128, 4096), BF),
            pltpu.VMEM((RAY, 48, 128), BF),
            pltpu.VMEM((RAY, 64, 128), BF),
            pltpu.VMEM((64, 128), F32),
            pltpu.VMEM((BRICK, 16, 16, 128), BF),
            pltpu.VMEM((BRICK, 16, 16, 128), BF),
            pltpu.VMEM((BRICK, 16, 128), BF),
            pltpu.VMEM((BRICK, 16, 128), BF),
            pltpu.VMEM((4, 8, 128), F32),
            pltpu.VMEM((4, 8, 128), F32),
            pltpu.VMEM((288, 128), F32),
            pltpu.VMEM((4, 72, 128), F32),
            dma((2,)),
            dma((BRICK,)),
            dma((BRICK,)),
            dma((BRICK,)),
            dma((RAY,)),
            dma((RAY,)),
            dma((4, RAY)),
            dma((4, RAY)),
            dma((BRICK,)),
            dma((BRICK,)),
            dma((BRICK,)),
            dma((BRICK,)),
            dma((BRICK,)),
            dma((BRICK,)),
            dma((2,)),
            dma((2,)),
        ],
        compiler_params=pltpu.CompilerParams(
            collective_id=0, has_side_effects=True, vmem_limit_bytes=48 * 1024 * 1024
        ),
    )(estimate, blocks, block_bundle, sinogram.reshape(32, 128))
    return restored, residual.reshape(sinogram.shape)


def solution(mesh):
    return jax.shard_map(
        shards,
        mesh=mesh,
        in_specs=(
            P(None, ("ray", "brick"), None),
            P("brick", "ray", None, None),
            P("brick", "ray"),
            P("brick", "ray", None, None),
        ),
        out_specs=(P(None, ("ray", "brick"), None), P("brick", "ray", None, None)),
        check_vma=False,
    )
```

```python
import jax
import jax.numpy as jnp
from jax import lax
from jax.experimental import pallas as pl
from jax.experimental.pallas import tpu as pltpu
from jax.sharding import PartitionSpec as P

RAY = 16
BRICK = 8
SWEEPS = 3
MESH = pl.DeviceIdType.MESH
BF = jnp.bfloat16
F32 = jnp.float32

step_size = 0.5
tv_step = 0.28
tv_weight = 0.5


def slot_offsets(m):
    third = (m + 2) // 4
    middle, last = third % 2, third // 2
    return (
        middle * (1 + 2 * (m % 2)) + 2 * last,
        middle * (m // 4) + (1 - middle) * (m % 2),
    )


def ring_step(g):
    middle = ((g + 1) // 2) % 2
    step = (2 + g + (g // 2) * (1 - 2 * (g % 2))) % 4
    return step, middle * (4 - g) + (1 - middle) * (6 - 2 * g), 1 + middle


def kernel(
    est_hbm, blocks_hbm, bundle_hbm, sino_hbm,
    out_ref, res_ref,
    bundles, est, sino, tiles, tmp, weights, meta, contrib, picked, mate_out, mate_in, grad_out, grad_in,
    halo_top, halo_low, est_edges, gathered, anchor,
    load_sem, weight_sem, tile_recv, mate_recv, send_sem, recv_sem,
):
    ray = lax.axis_index("ray")
    brick = lax.axis_index("brick")
    z, core = brick // 2, brick % 2
    mate = 2 * z + 1 - core

    def tile_row(m):
        dz, dc = slot_offsets(m)
        return ((z + dz) % 4) * 2 + (core + dc) % 2

    def remote(src, dst, send, recv, to_ray, to_brick):
        return pltpu.make_async_remote_copy(
            src_ref=src, dst_ref=dst, send_sem=send, recv_sem=recv,
            device_id={"ray": to_ray, "brick": to_brick}, device_id_type=MESH,
        )

    def wait_bytes(ref, sem):
        pltpu.make_async_copy(ref, ref, sem).wait()

    load_est = pltpu.make_async_copy(est_hbm, est, load_sem.at[0])
    load_sino = pltpu.make_async_copy(sino_hbm, sino, load_sem.at[1])
    load_bundle = pltpu.make_async_copy(bundle_hbm, bundles, load_sem.at[2])
    load_est.start()
    load_sino.start()
    load_bundle.start()

    def load_block(m, _):
        pltpu.make_async_copy(
            blocks_hbm.at[0, pl.ds(2 * tile_row(m), 2)], weights.at[m], weight_sem.at[m]
        ).start()
        return 0

    lax.fori_loop(0, BRICK, load_block, 0)

    barrier = pltpu.get_barrier_semaphore()

    def greet(to_ray, to_brick):
        pl.semaphore_signal(barrier, inc=1, device_id={"ray": to_ray, "brick": to_brick}, device_id_type=MESH)

    for m in range(1, BRICK):
        greet(ray, (brick + m) % BRICK)
    for d in range(1, RAY):
        greet((ray + d) % RAY, brick)

    @pl.when(brick == 0)
    def _():
        for b in range(4):
            greet((ray + RAY - 1) % RAY, 2 * b + 1)

    @pl.when(brick == BRICK - 1)
    def _():
        for b in range(4):
            greet((ray + 1) % RAY, 2 * b)

    lane = lax.broadcasted_iota(jnp.int32, (8, 128), 1)
    row = lax.broadcasted_iota(jnp.int32, (8, 128), 0)
    lane32 = lax.broadcasted_iota(jnp.int32, (32, 128), 1)

    load_est.wait()
    for s in range(4):
        even = est[s, pl.ds(0, 32, stride=2), :]
        odd = est[s, pl.ds(1, 32, stride=2), :]
        tmp[pl.ds(s, 32, stride=8), :] = jnp.where(lane32 < 64, even, pltpu.roll(odd, 64, 1))
        tmp[pl.ds(4 + s, 32, stride=8), :] = jnp.where(lane32 < 64, pltpu.roll(even, 64, 1), odd)
    tiles[0] = tmp[...].astype(BF).reshape(16, 16, 128)

    pl.semaphore_wait(barrier, BRICK - 1 + RAY - 1 + 1)

    remote(tiles.at[0], tiles.at[1], send_sem.at[0], tile_recv.at[1], ray, mate).start()
    for step, slot in ((1, 2), (3, 3), (2, 6)):
        to = ((z + 4 - step) % 4) * 2 + core
        remote(tiles.at[0], tiles.at[slot], send_sem.at[0], tile_recv.at[slot], ray, to).start()

    load_bundle.wait()
    row_keys = []
    lane_key = jnp.zeros((8, 128), F32)
    for m in range(BRICK):
        first = bundles[0, 2 * tile_row(m)].astype(F32)
        second = bundles[0, 2 * tile_row(m) + 1].astype(F32)
        both = jnp.where(row < 4, first, second)
        row_keys.append(both * 4.0 + (row % 4).astype(F32))
        lane_key = jnp.where((lane % 64) // 8 == m, jnp.where((lane // 4) % 2 == 0, first, second), lane_key)
    load_sino.wait()
    meta[0, 0:32, :] = sino[...].astype(BF)
    meta[0, 32:48, :] = jnp.concatenate([lane_key, lane_key], axis=0).astype(BF)
    for d in range(1, RAY):
        remote(meta.at[0], meta.at[RAY - d], send_sem.at[1], recv_sem.at[1], (ray + d) % RAY, brick).start()

    above = (brick + BRICK - 1) % BRICK
    above_ray = (ray + (brick + BRICK - 1) // BRICK + RAY - 1) % RAY
    below = (brick + 1) % BRICK
    below_ray = (ray + (brick + 1) // BRICK) % RAY
    remote(
        est.at[:, pl.ds(56, 8), :], est_edges.at[0], send_sem.at[2], recv_sem.at[2], below_ray, below
    ).start()
    remote(
        est.at[:, pl.ds(0, 8), :], est_edges.at[1], send_sem.at[2], recv_sem.at[2], above_ray, above
    ).start()

    def project(m, _):
        @pl.when(m > 0)
        def _():
            wait_bytes(tiles.at[m], tile_recv.at[m])

        @pl.when((m == 2) | (m == 3) | (m == 6))
        def _():
            slot = m + 2 - m // 6
            remote(tiles.at[m], tiles.at[slot], send_sem.at[0], tile_recv.at[slot], ray, mate).start()

        wait_bytes(weights.at[m], weight_sem.at[m])
        held = tiles[m].astype(F32)
        left = jnp.concatenate(
            [half for c in range(16) for half in (held[c, 0:8], held[c, 8:16])], axis=1
        ).astype(BF)
        full = lax.dot_general(
            left, weights[m].reshape(256, 4096), (((1,), (1,)), ((), ())), preferred_element_type=F32
        )
        picked[pl.ds(pl.multiple_of(m * 8, 8), 8), :] = jnp.where(row < 4, full[:, :128], full[:, 128:])

        @pl.when(m % 2 == 1)
        def _():
            at = pl.ds(pl.multiple_of((m // 2) * 16, 16), 16)
            contrib[0, at, :] = picked[at, :].astype(BF)
            for d in range(1, RAY):
                remote(
                    contrib.at[0, at], contrib.at[RAY - d, at], send_sem.at[3], recv_sem.at[3],
                    (ray + d) % RAY, brick,
                ).start()

        return 0

    lax.fori_loop(0, BRICK, project, 0)

    wait_bytes(meta.at[pl.ds(1, RAY - 1)], recv_sem.at[1])
    own_first = (ray * 32).astype(F32)
    for b in range(4):
        row_keys.append(own_first + (b * 8 + row).astype(F32))
    row_keys = jnp.concatenate(row_keys, axis=0)
    columns = []
    for q in range(RAY // 2):
        key = jnp.where(
            lane < 64, meta[2 * q, 32:48, :].astype(F32)[0:8], meta[2 * q + 1, 32:48, :].astype(F32)[0:8]
        ) * 4.0 + (lane % 4).astype(F32)
        columns.append(jnp.where(row_keys == jnp.concatenate([key] * 12, axis=0), 1.0, 0.0))
    row_all = lax.broadcasted_iota(jnp.int32, (96, 128), 0)
    for q in range(4):
        owner = (ray + 4 * q + lane // 32) % RAY
        key = (owner * 32 + lane % 32).astype(F32)
        hit = (row_keys == jnp.concatenate([key] * 12, axis=0)) & (row_all < 64)
        columns.append(jnp.where(hit, -1.0, 0.0))
    select = jnp.concatenate(columns, axis=1).astype(BF)
    sinos = meta[:, 0:32, :].reshape(512, 128)

    wait_bytes(contrib.at[pl.ds(1, RAY - 1)], recv_sem.at[3])
    right = jnp.concatenate([contrib[...].reshape(1024, 128), sinos], axis=0)
    resid = jnp.dot(select, right, preferred_element_type=F32)
    picked[...] = resid[0:64]
    res_ref[...] = resid[64:96] - sino[...]

    def backproject(t, _):
        pass_on = (t == 0) | ((t % 2 == 1) & (t < 7))
        g = jnp.where(pass_on, t + 1, t - 1) // 2
        dz, first, stride = ring_step(g)
        dc = jnp.where(pass_on, 1, 0)
        m = first + dc * stride
        mine = picked[pl.ds(pl.multiple_of(m * 8, 8), 8), :]
        left = jnp.concatenate(
            [jnp.where(row < 4, mine, 0.0), jnp.where(row < 4, 0.0, mine)], axis=1
        ).astype(BF)
        spread = jnp.dot(left, weights[m].reshape(256, 4096), preferred_element_type=F32)
        pieces = [
            jnp.concatenate(
                [spread[:, c * 256 : c * 256 + 128], spread[:, c * 256 + 128 : c * 256 + 256]], axis=0
            )
            for c in range(16)
        ]

        @pl.when(pass_on)
        def _():
            for c in range(16):
                mate_out[g, c] = pieces[c].astype(BF)
            remote(mate_out.at[g], mate_in.at[g], send_sem.at[4], mate_recv.at[g], ray, mate).start()

        @pl.when(jnp.logical_not(pass_on))
        def _():
            wait_bytes(mate_in.at[g], mate_recv.at[g])
            for c in range(16):
                grad_out[g, c] = (pieces[c] + mate_in[g, c].astype(F32)).astype(BF)
            target = ((z + dz) % 4) * 2 + core

            @pl.when(g < 3)
            def _():
                remote(grad_out.at[g], grad_in.at[g], send_sem.at[5], recv_sem.at[5], ray, target).start()

            remote(
                grad_out.at[g, 15], halo_top.at[z], send_sem.at[6], recv_sem.at[6],
                (ray + (target + 1) // BRICK) % RAY, (target + 1) % BRICK,
            ).start()
            remote(
                grad_out.at[g, 0], halo_low.at[z], send_sem.at[7], recv_sem.at[7],
                (ray + (target + BRICK - 1) // BRICK + RAY - 1) % RAY, (target + BRICK - 1) % BRICK,
            ).start()

        return 0

    lax.fori_loop(0, BRICK, backproject, 0)

    wait_bytes(est_edges, recv_sem.at[2])
    wait_bytes(grad_in, recv_sem.at[5])
    total = grad_out[3].astype(F32)
    for g in range(3):
        total += grad_in[g].astype(F32)
    gathered[16:272, :] = total.reshape(256, 128)
    wait_bytes(halo_top, recv_sem.at[6])
    wait_bytes(halo_low, recv_sem.at[7])
    gathered[0:16, :] = halo_top[...].astype(F32).sum(axis=0)
    gathered[272:288, :] = halo_low[...].astype(F32).sum(axis=0)

    lane36 = lax.broadcasted_iota(jnp.int32, (36, 128), 1)
    for s in range(4):
        one = gathered[pl.ds(s, 36, stride=8), :]
        two = gathered[pl.ds(4 + s, 36, stride=8), :]
        anchor[s, pl.ds(0, 36, stride=2), :] = jnp.where(lane36 < 64, one, pltpu.roll(two, 64, 1))
        anchor[s, pl.ds(1, 36, stride=2), :] = jnp.where(lane36 < 64, pltpu.roll(one, 64, 1), two)
    image = jnp.concatenate([est_edges[0, :, 4:8, :], est[...], est_edges[1, :, 0:4, :]], axis=1)
    start = image - step_size * anchor[...]

    shape = (4, 72, 128)
    rows = lax.broadcasted_iota(jnp.int32, shape, 1)
    lanes = lax.broadcasted_iota(jnp.int32, shape, 2)
    at_start = (ray == 0) & (brick == 0)
    at_end = (ray == RAY - 1) & (brick == BRICK - 1)
    above_image = (rows < 4) & at_start
    below_image = (rows >= 68) & at_end
    last_lane = lanes == 127
    first_lane = lanes == 0
    level = jnp.zeros((1, 72, 128), F32)

    start = jnp.where(below_image, 0.0, start)
    primal = start
    extra = start
    dual_y = dual_x = dual_z = None
    for sweep in range(SWEEPS):
        diff_y = pltpu.roll(extra, 71, 1) - extra
        diff_x = jnp.where(last_lane, 0.0, pltpu.roll(extra, 127, 2)) - extra
        diff_z = jnp.concatenate([extra[1:] - extra[:-1], level], axis=0)
        trial_y, trial_x, trial_z = tv_step * diff_y, tv_step * diff_x, tv_step * diff_z
        if sweep:
            trial_y, trial_x, trial_z = dual_y + trial_y, dual_x + trial_x, dual_z + trial_z
        norm = trial_y * trial_y + trial_x * trial_x + trial_z * trial_z
        shrink = lax.rsqrt(jnp.maximum(1.0, norm * (1.0 / (tv_weight * tv_weight))))
        dual_y = jnp.where(above_image, 0.0, trial_y * shrink)
        dual_x = trial_x * shrink
        dual_z = trial_z * shrink
        div = dual_y - pltpu.roll(dual_y, 1, 1)
        div += dual_x - jnp.where(first_lane, 0.0, pltpu.roll(dual_x, 1, 2))
        div += dual_z - jnp.concatenate([level, dual_z[:-1]], axis=0)
        updated = (primal + tv_step * div + tv_step * start) * (1.0 / (1.0 + tv_step))
        extra = jnp.where(below_image, 0.0, 2.0 * updated - primal)
        primal = updated
    out_ref[...] = primal[:, 4:68, :]

    wait_bytes(tiles.at[pl.ds(1, BRICK - 1)], send_sem.at[0])
    wait_bytes(meta.at[pl.ds(1, RAY - 1)], send_sem.at[1])
    wait_bytes(est_edges, send_sem.at[2])
    wait_bytes(contrib.at[pl.ds(1, RAY - 1)], send_sem.at[3])
    wait_bytes(mate_in, send_sem.at[4])
    wait_bytes(grad_in, send_sem.at[5])
    wait_bytes(halo_top, send_sem.at[6])
    wait_bytes(halo_low, send_sem.at[7])


def shards(estimate, blocks, block_bundle, sinogram):
    dma = pltpu.SemaphoreType.DMA
    inputs = (estimate, blocks, block_bundle, sinogram.reshape(32, 128))
    restored, residual = pl.pallas_call(
        kernel,
        out_shape=(
            jax.ShapeDtypeStruct((4, 64, 128), F32),
            jax.ShapeDtypeStruct((32, 128), F32),
        ),
        in_specs=[pl.BlockSpec(memory_space=pltpu.HBM)] * 4,
        out_specs=(pl.BlockSpec(memory_space=pltpu.VMEM), pl.BlockSpec(memory_space=pltpu.VMEM)),
        scratch_shapes=[
            pltpu.SMEM((1, 16), jnp.int32),
            pltpu.VMEM((4, 64, 128), F32),
            pltpu.VMEM((32, 128), F32),
            pltpu.VMEM((BRICK, 16, 16, 128), BF),
            pltpu.VMEM((256, 128), F32),
            pltpu.VMEM((BRICK, 2, 128, 4096), BF),
            pltpu.VMEM((RAY, 48, 128), BF),
            pltpu.VMEM((RAY, 64, 128), BF),
            pltpu.VMEM((64, 128), F32),
            pltpu.VMEM((4, 16, 16, 128), BF),
            pltpu.VMEM((4, 16, 16, 128), BF),
            pltpu.VMEM((4, 16, 16, 128), BF),
            pltpu.VMEM((3, 16, 16, 128), BF),
            pltpu.VMEM((4, 16, 128), BF),
            pltpu.VMEM((4, 16, 128), BF),
            pltpu.VMEM((2, 4, 8, 128), F32),
            pltpu.VMEM((288, 128), F32),
            pltpu.VMEM((4, 72, 128), F32),
            dma((3,)),
            dma((BRICK,)),
            dma((BRICK,)),
            dma((4,)),
            dma((8,)),
            dma((8,)),
        ],
        compiler_params=pltpu.CompilerParams(
            collective_id=0, has_side_effects=True, vmem_limit_bytes=48 * 1024 * 1024
        ),
    )(*(pltpu.with_memory_space_constraint(array, pltpu.HBM) for array in inputs))
    return restored, residual.reshape(sinogram.shape)


def solution(mesh):
    return jax.shard_map(
        shards,
        mesh=mesh,
        in_specs=(
            P(None, ("ray", "brick"), None),
            P("brick", "ray", None, None),
            P("brick", "ray"),
            P("brick", "ray", None, None),
        ),
        out_specs=(P(None, ("ray", "brick"), None), P("brick", "ray", None, None)),
        check_vma=False,
    )
```

```python
import jax
import jax.numpy as jnp
from jax import lax
from jax.experimental import pallas as pl
from jax.experimental.pallas import tpu as pltpu
from jax.sharding import PartitionSpec as P

RAY = 16
BRICK = 8
SWEEPS = 3
MESH = pl.DeviceIdType.MESH
BF = jnp.bfloat16
F32 = jnp.float32

step_size = 0.5
tv_step = 0.28
tv_weight = 0.5


def slot_offsets(m):
    third = (m + 2) // 4
    middle, last = third % 2, third // 2
    return (
        middle * (1 + 2 * (m % 2)) + 2 * last,
        middle * (m // 4) + (1 - middle) * (m % 2),
    )


RAY_STEPS = sorted(
    ((dx, dy) for dx in range(4) for dy in range(4) if dx or dy),
    key=lambda step: -(min(step[0], 4 - step[0]) + min(step[1], 4 - step[1])),
)


def ring_step(g):
    middle = ((g + 1) // 2) % 2
    step = (2 + g + (g // 2) * (1 - 2 * (g % 2))) % 4
    return step, middle * (4 - g) + (1 - middle) * (6 - 2 * g), 1 + middle


def kernel(
    est_hbm, blocks_hbm, bundle_hbm, sino_hbm,
    out_ref, res_ref,
    bundles, est, sino, tiles, tmp, weights, meta, contrib, picked, mate_out, mate_in, grad_out, grad_in,
    halo_top, halo_low, est_edges, gathered, anchor,
    load_sem, weight_sem, tile_recv, mate_recv, send_sem, recv_sem,
):
    ray = lax.axis_index("ray")
    brick = lax.axis_index("brick")
    z, core = brick // 2, brick % 2
    mate = 2 * z + 1 - core
    ray_x, ray_y = ray // 4, ray % 4

    def ray_peer(dx, dy):
        return ((ray_x + dx) % 4) * 4 + (ray_y + dy) % 4

    def ray_slot(dx, dy):
        return ((4 - dx) % 4) * 4 + (4 - dy) % 4

    def tile_row(m):
        dz, dc = slot_offsets(m)
        return ((z + dz) % 4) * 2 + (core + dc) % 2

    def remote(src, dst, send, recv, to_ray, to_brick):
        return pltpu.make_async_remote_copy(
            src_ref=src, dst_ref=dst, send_sem=send, recv_sem=recv,
            device_id={"ray": to_ray, "brick": to_brick}, device_id_type=MESH,
        )

    def wait_bytes(ref, sem):
        pltpu.make_async_copy(ref, ref, sem).wait()

    load_est = pltpu.make_async_copy(est_hbm, est, load_sem.at[0])
    load_sino = pltpu.make_async_copy(sino_hbm, sino, load_sem.at[1])
    load_bundle = pltpu.make_async_copy(bundle_hbm, bundles, load_sem.at[2])
    load_est.start()

    barrier = pltpu.get_barrier_semaphore()

    def greet(to_ray, to_brick):
        pl.semaphore_signal(barrier, inc=1, device_id={"ray": to_ray, "brick": to_brick}, device_id_type=MESH)

    for m in range(1, BRICK):
        greet(ray, (brick + m) % BRICK)
    for dx, dy in RAY_STEPS:
        greet(ray_peer(dx, dy), brick)

    @pl.when(brick == 0)
    def _():
        for b in range(4):
            greet((ray + RAY - 1) % RAY, 2 * b + 1)

    @pl.when(brick == BRICK - 1)
    def _():
        for b in range(4):
            greet((ray + 1) % RAY, 2 * b)

    load_sino.start()
    load_bundle.start()

    def load_block(m, _):
        pltpu.make_async_copy(
            blocks_hbm.at[0, pl.ds(2 * tile_row(m), 2)], weights.at[m], weight_sem.at[m]
        ).start()
        return 0

    lax.fori_loop(0, BRICK, load_block, 0)

    lane = lax.broadcasted_iota(jnp.int32, (8, 128), 1)
    row = lax.broadcasted_iota(jnp.int32, (8, 128), 0)
    lane32 = lax.broadcasted_iota(jnp.int32, (32, 128), 1)

    load_est.wait()
    for s in range(4):
        even = est[s, pl.ds(0, 32, stride=2), :]
        odd = est[s, pl.ds(1, 32, stride=2), :]
        tmp[pl.ds(s, 32, stride=8), :] = jnp.where(lane32 < 64, even, pltpu.roll(odd, 64, 1))
        tmp[pl.ds(4 + s, 32, stride=8), :] = jnp.where(lane32 < 64, pltpu.roll(even, 64, 1), odd)
    tiles[0] = tmp[...].astype(BF).reshape(16, 16, 128)

    pl.semaphore_wait(barrier, BRICK - 1 + RAY - 1 + 1)

    remote(tiles.at[0], tiles.at[1], send_sem.at[0], tile_recv.at[1], ray, mate).start()
    for step, slot in ((1, 2), (3, 3), (2, 6)):
        to = ((z + 4 - step) % 4) * 2 + core
        remote(tiles.at[0], tiles.at[slot], send_sem.at[0], tile_recv.at[slot], ray, to).start()

    load_bundle.wait()
    row_keys = []
    lane_key = jnp.zeros((8, 128), F32)
    for m in range(BRICK):
        first = bundles[0, 2 * tile_row(m)].astype(F32)
        second = bundles[0, 2 * tile_row(m) + 1].astype(F32)
        both = jnp.where(row < 4, first, second)
        row_keys.append(both * 4.0 + (row % 4).astype(F32))
        lane_key = jnp.where((lane % 64) // 8 == m, jnp.where((lane // 4) % 2 == 0, first, second), lane_key)
    load_sino.wait()
    meta[0, 0:32, :] = sino[...].astype(BF)
    meta[0, 32:48, :] = jnp.concatenate([lane_key, lane_key], axis=0).astype(BF)
    for dx, dy in RAY_STEPS:
        remote(
            meta.at[0], meta.at[ray_slot(dx, dy)], send_sem.at[1], recv_sem.at[1], ray_peer(dx, dy), brick
        ).start()

    above = (brick + BRICK - 1) % BRICK
    above_ray = (ray + (brick + BRICK - 1) // BRICK + RAY - 1) % RAY
    below = (brick + 1) % BRICK
    below_ray = (ray + (brick + 1) // BRICK) % RAY
    remote(
        est.at[:, pl.ds(56, 8), :], est_edges.at[0], send_sem.at[2], recv_sem.at[2], below_ray, below
    ).start()
    remote(
        est.at[:, pl.ds(0, 8), :], est_edges.at[1], send_sem.at[2], recv_sem.at[2], above_ray, above
    ).start()

    def project(m, _):
        @pl.when(m > 0)
        def _():
            wait_bytes(tiles.at[m], tile_recv.at[m])

        @pl.when((m == 2) | (m == 3) | (m == 6))
        def _():
            slot = m + 2 - m // 6
            remote(tiles.at[m], tiles.at[slot], send_sem.at[0], tile_recv.at[slot], ray, mate).start()

        wait_bytes(weights.at[m], weight_sem.at[m])
        held = tiles[m].astype(F32)
        left = jnp.concatenate(
            [half for c in range(16) for half in (held[c, 0:8], held[c, 8:16])], axis=1
        ).astype(BF)
        full = lax.dot_general(
            left, weights[m].reshape(256, 4096), (((1,), (1,)), ((), ())), preferred_element_type=F32
        )
        picked[pl.ds(pl.multiple_of(m * 8, 8), 8), :] = jnp.where(row < 4, full[:, :128], full[:, 128:])

        def hand_out(at):
            contrib[0, at, :] = picked[at, :].astype(BF)
            for dx, dy in RAY_STEPS:
                remote(
                    contrib.at[0, at], contrib.at[ray_slot(dx, dy), at], send_sem.at[3], recv_sem.at[3],
                    ray_peer(dx, dy), brick,
                ).start()

        pl.when(m == 5)(lambda: hand_out(pl.ds(0, 48)))
        pl.when(m == 7)(lambda: hand_out(pl.ds(48, 16)))
        return 0

    lax.fori_loop(0, BRICK, project, 0)

    wait_bytes(meta.at[pl.ds(1, RAY - 1)], recv_sem.at[1])
    own_first = (ray * 32).astype(F32)
    for b in range(4):
        row_keys.append(own_first + (b * 8 + row).astype(F32))
    row_keys = jnp.concatenate(row_keys, axis=0)
    columns = []
    for q in range(RAY // 2):
        key = jnp.where(
            lane < 64, meta[2 * q, 32:48, :].astype(F32)[0:8], meta[2 * q + 1, 32:48, :].astype(F32)[0:8]
        ) * 4.0 + (lane % 4).astype(F32)
        columns.append(jnp.where(row_keys == jnp.concatenate([key] * 12, axis=0), 1.0, 0.0))
    row_all = lax.broadcasted_iota(jnp.int32, (96, 128), 0)
    for q in range(4):
        owner = ((ray_x + q) % 4) * 4 + (ray_y + lane // 32) % 4
        key = (owner * 32 + lane % 32).astype(F32)
        hit = (row_keys == jnp.concatenate([key] * 12, axis=0)) & (row_all < 64)
        columns.append(jnp.where(hit, -1.0, 0.0))
    select = jnp.concatenate(columns, axis=1).astype(BF)
    sinos = meta[:, 0:32, :].reshape(512, 128)

    wait_bytes(contrib.at[pl.ds(1, RAY - 1)], recv_sem.at[3])
    right = jnp.concatenate([contrib[...].reshape(1024, 128), sinos], axis=0)
    resid = jnp.dot(select, right, preferred_element_type=F32)
    picked[...] = resid[0:64]
    res_ref[...] = resid[64:96] - sino[...]

    def backproject(t, _):
        pass_on = (t == 0) | ((t % 2 == 1) & (t < 7))
        g = jnp.where(pass_on, t + 1, t - 1) // 2
        dz, first, stride = ring_step(g)
        dc = jnp.where(pass_on, 1, 0)
        m = first + dc * stride
        mine = picked[pl.ds(pl.multiple_of(m * 8, 8), 8), :]
        left = jnp.concatenate(
            [jnp.where(row < 4, mine, 0.0), jnp.where(row < 4, 0.0, mine)], axis=1
        ).astype(BF)
        spread = jnp.dot(left, weights[m].reshape(256, 4096), preferred_element_type=F32)
        pieces = [
            jnp.concatenate(
                [spread[:, c * 256 : c * 256 + 128], spread[:, c * 256 + 128 : c * 256 + 256]], axis=0
            )
            for c in range(16)
        ]

        @pl.when(pass_on)
        def _():
            for c in range(16):
                mate_out[g, c] = pieces[c].astype(BF)
            remote(mate_out.at[g], mate_in.at[g], send_sem.at[4], mate_recv.at[g], ray, mate).start()

        @pl.when(jnp.logical_not(pass_on))
        def _():
            wait_bytes(mate_in.at[g], mate_recv.at[g])
            for c in range(16):
                grad_out[g, c] = (pieces[c] + mate_in[g, c].astype(F32)).astype(BF)
            target = ((z + dz) % 4) * 2 + core

            @pl.when(g < 3)
            def _():
                remote(grad_out.at[g], grad_in.at[g], send_sem.at[5], recv_sem.at[5], ray, target).start()

            remote(
                grad_out.at[g, 15], halo_top.at[z], send_sem.at[6], recv_sem.at[6],
                (ray + (target + 1) // BRICK) % RAY, (target + 1) % BRICK,
            ).start()
            remote(
                grad_out.at[g, 0], halo_low.at[z], send_sem.at[7], recv_sem.at[7],
                (ray + (target + BRICK - 1) // BRICK + RAY - 1) % RAY, (target + BRICK - 1) % BRICK,
            ).start()

        return 0

    lax.fori_loop(0, BRICK, backproject, 0)

    wait_bytes(est_edges, recv_sem.at[2])
    wait_bytes(grad_in, recv_sem.at[5])
    total = grad_out[3].astype(F32)
    for g in range(3):
        total += grad_in[g].astype(F32)
    gathered[16:272, :] = total.reshape(256, 128)
    wait_bytes(halo_top, recv_sem.at[6])
    wait_bytes(halo_low, recv_sem.at[7])
    gathered[0:16, :] = halo_top[...].astype(F32).sum(axis=0)
    gathered[272:288, :] = halo_low[...].astype(F32).sum(axis=0)

    lane36 = lax.broadcasted_iota(jnp.int32, (36, 128), 1)
    for s in range(4):
        one = gathered[pl.ds(s, 36, stride=8), :]
        two = gathered[pl.ds(4 + s, 36, stride=8), :]
        anchor[s, pl.ds(0, 36, stride=2), :] = jnp.where(lane36 < 64, one, pltpu.roll(two, 64, 1))
        anchor[s, pl.ds(1, 36, stride=2), :] = jnp.where(lane36 < 64, pltpu.roll(one, 64, 1), two)
    image = jnp.concatenate([est_edges[0, :, 4:8, :], est[...], est_edges[1, :, 0:4, :]], axis=1)
    start = image - step_size * anchor[...]

    out_ref[...] = start

    wait_bytes(tiles.at[pl.ds(1, BRICK - 1)], send_sem.at[0])
    wait_bytes(meta.at[pl.ds(1, RAY - 1)], send_sem.at[1])
    wait_bytes(est_edges, send_sem.at[2])
    wait_bytes(contrib.at[pl.ds(1, RAY - 1)], send_sem.at[3])
    wait_bytes(mate_in, send_sem.at[4])
    wait_bytes(grad_in, send_sem.at[5])
    wait_bytes(halo_top, send_sem.at[6])
    wait_bytes(halo_low, send_sem.at[7])


def sweeps_kernel(start_ref, res_ref, out_hbm, res_hbm, out, save_sem):
    ray = lax.axis_index("ray")
    brick = lax.axis_index("brick")
    save_res = pltpu.make_async_copy(res_ref, res_hbm, save_sem.at[0])
    save_out = pltpu.make_async_copy(out, out_hbm, save_sem.at[1])
    save_res.start()

    shape = (4, 72, 128)
    rows = lax.broadcasted_iota(jnp.int32, shape, 1)
    lanes = lax.broadcasted_iota(jnp.int32, shape, 2)
    at_start = (ray == 0) & (brick == 0)
    at_end = (ray == RAY - 1) & (brick == BRICK - 1)
    above_image = (rows < 4) & at_start
    below_image = (rows >= 68) & at_end
    last_lane = lanes == 127
    first_lane = lanes == 0
    level = jnp.zeros((1, 72, 128), F32)

    start = jnp.where(below_image, 0.0, start_ref[...])
    primal = start
    extra = start
    dual_y = dual_x = dual_z = None
    for sweep in range(SWEEPS):
        diff_y = pltpu.roll(extra, 71, 1) - extra
        diff_x = jnp.where(last_lane, 0.0, pltpu.roll(extra, 127, 2)) - extra
        diff_z = jnp.concatenate([extra[1:] - extra[:-1], level], axis=0)
        trial_y, trial_x, trial_z = tv_step * diff_y, tv_step * diff_x, tv_step * diff_z
        if sweep:
            trial_y, trial_x, trial_z = dual_y + trial_y, dual_x + trial_x, dual_z + trial_z
        norm = trial_y * trial_y + trial_x * trial_x + trial_z * trial_z
        shrink = lax.rsqrt(jnp.maximum(1.0, norm * (1.0 / (tv_weight * tv_weight))))
        dual_y = jnp.where(above_image, 0.0, trial_y * shrink)
        dual_x = trial_x * shrink
        dual_z = trial_z * shrink
        div = dual_y - pltpu.roll(dual_y, 1, 1)
        div += dual_x - jnp.where(first_lane, 0.0, pltpu.roll(dual_x, 1, 2))
        div += dual_z - jnp.concatenate([level, dual_z[:-1]], axis=0)
        updated = (primal + tv_step * div + tv_step * start) * (1.0 / (1.0 + tv_step))
        extra = jnp.where(below_image, 0.0, 2.0 * updated - primal)
        primal = updated
    out[...] = primal[:, 4:68, :]
    save_out.start()
    save_res.wait()
    save_out.wait()


def shards(estimate, blocks, block_bundle, sinogram):
    dma = pltpu.SemaphoreType.DMA
    inputs = (estimate, blocks, block_bundle, sinogram.reshape(32, 128))
    start, residual = pl.pallas_call(
        kernel,
        out_shape=(
            jax.ShapeDtypeStruct((4, 72, 128), F32),
            jax.ShapeDtypeStruct((32, 128), F32),
        ),
        in_specs=[pl.BlockSpec(memory_space=pltpu.HBM)] * 4,
        out_specs=(pl.BlockSpec(memory_space=pltpu.VMEM), pl.BlockSpec(memory_space=pltpu.VMEM)),
        scratch_shapes=[
            pltpu.SMEM((1, 16), jnp.int32),
            pltpu.VMEM((4, 64, 128), F32),
            pltpu.VMEM((32, 128), F32),
            pltpu.VMEM((BRICK, 16, 16, 128), BF),
            pltpu.VMEM((256, 128), F32),
            pltpu.VMEM((BRICK, 2, 128, 4096), BF),
            pltpu.VMEM((RAY, 48, 128), BF),
            pltpu.VMEM((RAY, 64, 128), BF),
            pltpu.VMEM((64, 128), F32),
            pltpu.VMEM((4, 16, 16, 128), BF),
            pltpu.VMEM((4, 16, 16, 128), BF),
            pltpu.VMEM((4, 16, 16, 128), BF),
            pltpu.VMEM((3, 16, 16, 128), BF),
            pltpu.VMEM((4, 16, 128), BF),
            pltpu.VMEM((4, 16, 128), BF),
            pltpu.VMEM((2, 4, 8, 128), F32),
            pltpu.VMEM((288, 128), F32),
            pltpu.VMEM((4, 72, 128), F32),
            dma((3,)),
            dma((BRICK,)),
            dma((BRICK,)),
            dma((4,)),
            dma((8,)),
            dma((8,)),
        ],
        compiler_params=pltpu.CompilerParams(
            collective_id=0, has_side_effects=True, vmem_limit_bytes=48 * 1024 * 1024
        ),
    )(*(pltpu.with_memory_space_constraint(array, pltpu.HBM) for array in inputs))
    restored, residual = pl.pallas_call(
        sweeps_kernel,
        out_shape=(
            jax.ShapeDtypeStruct((4, 64, 128), F32),
            jax.ShapeDtypeStruct((32, 128), F32),
        ),
        in_specs=[pl.BlockSpec(memory_space=pltpu.VMEM)] * 2,
        out_specs=(pl.BlockSpec(memory_space=pltpu.HBM),) * 2,
        scratch_shapes=[pltpu.VMEM((4, 64, 128), F32), dma((2,))],
        compiler_params=pltpu.CompilerParams(vmem_limit_bytes=16 * 1024 * 1024),
    )(start, residual)
    return restored, residual.reshape(sinogram.shape)


def solution(mesh):
    return jax.shard_map(
        shards,
        mesh=mesh,
        in_specs=(
            P(None, ("ray", "brick"), None),
            P("brick", "ray", None, None),
            P("brick", "ray"),
            P("brick", "ray", None, None),
        ),
        out_specs=(P(None, ("ray", "brick"), None), P("brick", "ray", None, None)),
        check_vma=False,
    )
```

```python
import jax
import jax.numpy as jnp
from jax import lax
from jax.experimental import pallas as pl
from jax.experimental.pallas import tpu as pltpu
from jax.sharding import PartitionSpec as P

RAY = 16
BRICK = 8
SWEEPS = 3
MESH = pl.DeviceIdType.MESH
BF = jnp.bfloat16
F32 = jnp.float32

step_size = 0.5
tv_step = 0.28
tv_weight = 0.5


def slot_offsets(m):
    third = (m + 2) // 4
    middle, last = third % 2, third // 2
    return (
        middle * (1 + 2 * (m % 2)) + 2 * last,
        middle * (m // 4) + (1 - middle) * (m % 2),
    )


RAY_STEPS = sorted(
    ((dx, dy) for dx in range(4) for dy in range(4) if dx or dy),
    key=lambda step: -(min(step[0], 4 - step[0]) + min(step[1], 4 - step[1])),
)


def ring_step(g):
    middle = ((g + 1) // 2) % 2
    step = (2 + g + (g // 2) * (1 - 2 * (g % 2))) % 4
    return step, middle * (4 - g) + (1 - middle) * (6 - 2 * g), 1 + middle


def kernel(
    est_hbm, blocks_hbm, bundle_hbm, sino_hbm,
    out_ref, res_ref,
    bundles, est, sino, tiles, tmp, weights, meta, contrib, picked, mate_out, mate_in, grad_out, grad_in,
    halo_top, halo_low, far_out, far_in, est_edges, gathered, anchor,
    load_sem, weight_sem, tile_recv, mate_recv, send_sem, recv_sem,
):
    ray = lax.axis_index("ray")
    brick = lax.axis_index("brick")
    z, core = brick // 2, brick % 2
    mate = 2 * z + 1 - core
    ray_x, ray_y = ray // 4, ray % 4

    def ray_peer(dx, dy):
        return ((ray_x + dx) % 4) * 4 + (ray_y + dy) % 4

    def ray_slot(dx, dy):
        return ((4 - dx) % 4) * 4 + (4 - dy) % 4

    def tile_row(m):
        dz, dc = slot_offsets(m)
        return ((z + dz) % 4) * 2 + (core + dc) % 2

    def remote(src, dst, send, recv, to_ray, to_brick):
        return pltpu.make_async_remote_copy(
            src_ref=src, dst_ref=dst, send_sem=send, recv_sem=recv,
            device_id={"ray": to_ray, "brick": to_brick}, device_id_type=MESH,
        )

    def wait_bytes(ref, sem):
        pltpu.make_async_copy(ref, ref, sem).wait()

    load_est = pltpu.make_async_copy(est_hbm, est, load_sem.at[0])
    load_sino = pltpu.make_async_copy(sino_hbm, sino, load_sem.at[1])
    load_bundle = pltpu.make_async_copy(bundle_hbm, bundles, load_sem.at[2])
    load_est.start()

    barrier = pltpu.get_barrier_semaphore()

    def greet(to_ray, to_brick):
        pl.semaphore_signal(barrier, inc=1, device_id={"ray": to_ray, "brick": to_brick}, device_id_type=MESH)

    for m in range(1, BRICK):
        greet(ray, (brick + m) % BRICK)
    for dx, dy in RAY_STEPS:
        greet(ray_peer(dx, dy), brick)

    @pl.when(brick == 0)
    def _():
        for b in range(BRICK):
            greet((ray + RAY - 1) % RAY, b)

    @pl.when(brick == BRICK - 1)
    def _():
        for b in range(BRICK):
            greet((ray + 1) % RAY, b)

    load_sino.start()
    load_bundle.start()

    def load_block(m, _):
        pltpu.make_async_copy(
            blocks_hbm.at[0, pl.ds(2 * tile_row(m), 2)], weights.at[m], weight_sem.at[m]
        ).start()
        return 0

    lax.fori_loop(0, BRICK, load_block, 0)

    lane = lax.broadcasted_iota(jnp.int32, (8, 128), 1)
    row = lax.broadcasted_iota(jnp.int32, (8, 128), 0)
    lane32 = lax.broadcasted_iota(jnp.int32, (32, 128), 1)

    load_est.wait()
    for s in range(4):
        even = est[s, pl.ds(0, 32, stride=2), :]
        odd = est[s, pl.ds(1, 32, stride=2), :]
        tmp[pl.ds(s, 32, stride=8), :] = jnp.where(lane32 < 64, even, pltpu.roll(odd, 64, 1))
        tmp[pl.ds(4 + s, 32, stride=8), :] = jnp.where(lane32 < 64, pltpu.roll(even, 64, 1), odd)
    tiles[0] = tmp[...].astype(BF).reshape(16, 16, 128)

    pl.semaphore_wait(barrier, BRICK - 1 + RAY - 1 + 2)

    remote(tiles.at[0], tiles.at[1], send_sem.at[0], tile_recv.at[1], ray, mate).start()
    for step, slot in ((1, 2), (3, 3), (2, 6)):
        to = ((z + 4 - step) % 4) * 2 + core
        remote(tiles.at[0], tiles.at[slot], send_sem.at[0], tile_recv.at[slot], ray, to).start()

    load_bundle.wait()
    row_keys = []
    lane_key = jnp.zeros((8, 128), F32)
    for m in range(BRICK):
        first = bundles[0, 2 * tile_row(m)].astype(F32)
        second = bundles[0, 2 * tile_row(m) + 1].astype(F32)
        both = jnp.where(row < 4, first, second)
        row_keys.append(both * 4.0 + (row % 4).astype(F32))
        lane_key = jnp.where((lane % 64) // 8 == m, jnp.where((lane // 4) % 2 == 0, first, second), lane_key)
    load_sino.wait()
    meta[0, 0:32, :] = sino[...].astype(BF)
    meta[0, 32:48, :] = jnp.concatenate([lane_key, lane_key], axis=0).astype(BF)
    for dx, dy in RAY_STEPS:
        remote(
            meta.at[0], meta.at[ray_slot(dx, dy)], send_sem.at[1], recv_sem.at[1], ray_peer(dx, dy), brick
        ).start()

    above = (brick + BRICK - 1) % BRICK
    above_ray = (ray + (brick + BRICK - 1) // BRICK + RAY - 1) % RAY
    below = (brick + 1) % BRICK
    below_ray = (ray + (brick + 1) // BRICK) % RAY
    remote(
        est.at[:, pl.ds(56, 8), :], est_edges.at[0], send_sem.at[2], recv_sem.at[2], below_ray, below
    ).start()
    remote(
        est.at[:, pl.ds(0, 8), :], est_edges.at[1], send_sem.at[2], recv_sem.at[2], above_ray, above
    ).start()

    def project(m, _):
        @pl.when(m > 0)
        def _():
            wait_bytes(tiles.at[m], tile_recv.at[m])

        @pl.when((m == 2) | (m == 3) | (m == 6))
        def _():
            slot = m + 2 - m // 6
            remote(tiles.at[m], tiles.at[slot], send_sem.at[0], tile_recv.at[slot], ray, mate).start()

        wait_bytes(weights.at[m], weight_sem.at[m])
        held = tiles[m].astype(F32)
        left = jnp.concatenate(
            [half for c in range(16) for half in (held[c, 0:8], held[c, 8:16])], axis=1
        ).astype(BF)
        full = lax.dot_general(
            left, weights[m].reshape(256, 4096), (((1,), (1,)), ((), ())), preferred_element_type=F32
        )
        picked[pl.ds(pl.multiple_of(m * 8, 8), 8), :] = jnp.where(row < 4, full[:, :128], full[:, 128:])

        def hand_out(at):
            contrib[0, at, :] = picked[at, :].astype(BF)
            for dx, dy in RAY_STEPS:
                remote(
                    contrib.at[0, at], contrib.at[ray_slot(dx, dy), at], send_sem.at[3], recv_sem.at[3],
                    ray_peer(dx, dy), brick,
                ).start()

        pl.when(m == 5)(lambda: hand_out(pl.ds(0, 48)))
        pl.when(m == 7)(lambda: hand_out(pl.ds(48, 16)))
        return 0

    lax.fori_loop(0, BRICK, project, 0)

    wait_bytes(meta.at[pl.ds(1, RAY - 1)], recv_sem.at[1])
    own_first = (ray * 32).astype(F32)
    for b in range(4):
        row_keys.append(own_first + (b * 8 + row).astype(F32))
    row_keys = jnp.concatenate(row_keys, axis=0)
    columns = []
    for q in range(RAY // 2):
        key = jnp.where(
            lane < 64, meta[2 * q, 32:48, :].astype(F32)[0:8], meta[2 * q + 1, 32:48, :].astype(F32)[0:8]
        ) * 4.0 + (lane % 4).astype(F32)
        columns.append(jnp.where(row_keys == jnp.concatenate([key] * 12, axis=0), 1.0, 0.0))
    row_all = lax.broadcasted_iota(jnp.int32, (96, 128), 0)
    for q in range(4):
        owner = ((ray_x + q) % 4) * 4 + (ray_y + lane // 32) % 4
        key = (owner * 32 + lane % 32).astype(F32)
        hit = (row_keys == jnp.concatenate([key] * 12, axis=0)) & (row_all < 64)
        columns.append(jnp.where(hit, -1.0, 0.0))
    select = jnp.concatenate(columns, axis=1).astype(BF)
    sinos = meta[:, 0:32, :].reshape(512, 128)

    wait_bytes(contrib.at[pl.ds(1, RAY - 1)], recv_sem.at[3])
    right = jnp.concatenate([contrib[...].reshape(1024, 128), sinos], axis=0)
    resid = jnp.dot(select, right, preferred_element_type=F32)
    picked[...] = resid[0:64]
    res_ref[...] = resid[64:96] - sino[...]

    def split_left(m):
        mine = picked[pl.ds(pl.multiple_of(m * 8, 8), 8), :]
        return jnp.concatenate(
            [jnp.where(row < 4, mine, 0.0), jnp.where(row < 4, 0.0, mine)], axis=1
        ).astype(BF)

    for edge, (last, column) in enumerate(((BRICK - 1, 15), (0, 0))):
        dz = (last // 2 + 4 - z) % 4
        dc = (last + core) % 2
        odd = dz % 2
        m = odd * (2 + dz // 2 + 2 * dc) + (1 - odd) * (3 * dz + dc)
        rim = jnp.dot(
            split_left(m),
            weights[m, :, :, column * 256 : column * 256 + 256].reshape(256, 256),
            preferred_element_type=F32,
        )
        far_out[edge] = jnp.concatenate([rim[:, :128], rim[:, 128:]], axis=0).astype(BF)
        remote(
            far_out.at[edge], far_in.at[brick], send_sem.at[7], recv_sem.at[7],
            (ray + (1, RAY - 1)[edge]) % RAY, (0, BRICK - 1)[edge],
        ).start()

    def backproject(t, _):
        pass_on = (t == 0) | ((t % 2 == 1) & (t < 7))
        g = jnp.where(pass_on, t + 1, t - 1) // 2
        dz, first, stride = ring_step(g)
        dc = jnp.where(pass_on, 1, 0)
        m = first + dc * stride
        spread = jnp.dot(split_left(m), weights[m].reshape(256, 4096), preferred_element_type=F32)
        pieces = [
            jnp.concatenate(
                [spread[:, c * 256 : c * 256 + 128], spread[:, c * 256 + 128 : c * 256 + 256]], axis=0
            )
            for c in range(16)
        ]

        @pl.when(pass_on)
        def _():
            for c in range(16):
                mate_out[g, c] = pieces[c].astype(BF)
            remote(mate_out.at[g], mate_in.at[g], send_sem.at[4], mate_recv.at[g], ray, mate).start()

        @pl.when(jnp.logical_not(pass_on))
        def _():
            wait_bytes(mate_in.at[g], mate_recv.at[g])
            for c in range(16):
                grad_out[g, c] = (pieces[c] + mate_in[g, c].astype(F32)).astype(BF)
            target = ((z + dz) % 4) * 2 + core

            @pl.when(g < 3)
            def _():
                remote(grad_out.at[g], grad_in.at[g], send_sem.at[5], recv_sem.at[5], ray, target).start()

            @pl.when(target < BRICK - 1)
            def _():
                remote(
                    grad_out.at[g, 15], halo_top.at[z], send_sem.at[6], recv_sem.at[6], ray, target + 1
                ).start()

            @pl.when(target > 0)
            def _():
                remote(
                    grad_out.at[g, 0], halo_low.at[z], send_sem.at[6], recv_sem.at[8], ray, target - 1
                ).start()

        return 0

    lax.fori_loop(0, BRICK, backproject, 0)

    wait_bytes(est_edges, recv_sem.at[2])
    wait_bytes(grad_in, recv_sem.at[5])
    total = grad_out[3].astype(F32)
    for g in range(3):
        total += grad_in[g].astype(F32)
    gathered[16:272, :] = total.reshape(256, 128)

    @pl.when(brick > 0)
    def _():
        wait_bytes(halo_top, recv_sem.at[6])
        gathered[0:16, :] = halo_top[...].astype(F32).sum(axis=0)

    @pl.when(brick < BRICK - 1)
    def _():
        wait_bytes(halo_low, recv_sem.at[8])
        gathered[272:288, :] = halo_low[...].astype(F32).sum(axis=0)

    @pl.when(brick == 0)
    def _():
        wait_bytes(far_in, recv_sem.at[7])
        gathered[0:16, :] = far_in[...].astype(F32).sum(axis=0)

    @pl.when(brick == BRICK - 1)
    def _():
        wait_bytes(far_in, recv_sem.at[7])
        gathered[272:288, :] = far_in[...].astype(F32).sum(axis=0)

    lane36 = lax.broadcasted_iota(jnp.int32, (36, 128), 1)
    for s in range(4):
        one = gathered[pl.ds(s, 36, stride=8), :]
        two = gathered[pl.ds(4 + s, 36, stride=8), :]
        anchor[s, pl.ds(0, 36, stride=2), :] = jnp.where(lane36 < 64, one, pltpu.roll(two, 64, 1))
        anchor[s, pl.ds(1, 36, stride=2), :] = jnp.where(lane36 < 64, pltpu.roll(one, 64, 1), two)
    image = jnp.concatenate([est_edges[0, :, 4:8, :], est[...], est_edges[1, :, 0:4, :]], axis=1)
    start = image - step_size * anchor[...]

    out_ref[...] = start

    wait_bytes(tiles.at[pl.ds(1, BRICK - 1)], send_sem.at[0])
    wait_bytes(meta.at[pl.ds(1, RAY - 1)], send_sem.at[1])
    wait_bytes(est_edges, send_sem.at[2])
    wait_bytes(contrib.at[pl.ds(1, RAY - 1)], send_sem.at[3])
    wait_bytes(mate_in, send_sem.at[4])
    wait_bytes(grad_in, send_sem.at[5])
    wait_bytes(tiles.at[0, pl.ds(0, 7)], send_sem.at[6])
    wait_bytes(far_out, send_sem.at[7])


def sweeps_kernel(start_ref, res_ref, out_hbm, res_hbm, out, save_sem):
    ray = lax.axis_index("ray")
    brick = lax.axis_index("brick")
    save_res = pltpu.make_async_copy(res_ref, res_hbm, save_sem.at[0])
    save_out = pltpu.make_async_copy(out, out_hbm, save_sem.at[1])
    save_res.start()

    shape = (4, 72, 128)
    rows = lax.broadcasted_iota(jnp.int32, shape, 1)
    lanes = lax.broadcasted_iota(jnp.int32, shape, 2)
    at_start = (ray == 0) & (brick == 0)
    at_end = (ray == RAY - 1) & (brick == BRICK - 1)
    above_image = (rows < 4) & at_start
    below_image = (rows >= 68) & at_end
    last_lane = lanes == 127
    first_lane = lanes == 0
    level = jnp.zeros((1, 72, 128), F32)

    start = jnp.where(below_image, 0.0, start_ref[...])
    primal = start
    extra = start
    dual_y = dual_x = dual_z = None
    for sweep in range(SWEEPS):
        diff_y = pltpu.roll(extra, 71, 1) - extra
        diff_x = jnp.where(last_lane, 0.0, pltpu.roll(extra, 127, 2)) - extra
        diff_z = jnp.concatenate([extra[1:] - extra[:-1], level], axis=0)
        trial_y, trial_x, trial_z = tv_step * diff_y, tv_step * diff_x, tv_step * diff_z
        if sweep:
            trial_y, trial_x, trial_z = dual_y + trial_y, dual_x + trial_x, dual_z + trial_z
        norm = trial_y * trial_y + trial_x * trial_x + trial_z * trial_z
        shrink = lax.rsqrt(jnp.maximum(1.0, norm * (1.0 / (tv_weight * tv_weight))))
        dual_y = jnp.where(above_image, 0.0, trial_y * shrink)
        dual_x = trial_x * shrink
        dual_z = trial_z * shrink
        div = dual_y - pltpu.roll(dual_y, 1, 1)
        div += dual_x - jnp.where(first_lane, 0.0, pltpu.roll(dual_x, 1, 2))
        div += dual_z - jnp.concatenate([level, dual_z[:-1]], axis=0)
        updated = (primal + tv_step * div + tv_step * start) * (1.0 / (1.0 + tv_step))
        extra = jnp.where(below_image, 0.0, 2.0 * updated - primal)
        primal = updated
    out[...] = primal[:, 4:68, :]
    save_out.start()
    save_res.wait()
    save_out.wait()


def shards(estimate, blocks, block_bundle, sinogram):
    dma = pltpu.SemaphoreType.DMA
    inputs = (estimate, blocks, block_bundle, sinogram.reshape(32, 128))
    start, residual = pl.pallas_call(
        kernel,
        out_shape=(
            jax.ShapeDtypeStruct((4, 72, 128), F32),
            jax.ShapeDtypeStruct((32, 128), F32),
        ),
        in_specs=[pl.BlockSpec(memory_space=pltpu.HBM)] * 4,
        out_specs=(pl.BlockSpec(memory_space=pltpu.VMEM), pl.BlockSpec(memory_space=pltpu.VMEM)),
        scratch_shapes=[
            pltpu.SMEM((1, 16), jnp.int32),
            pltpu.VMEM((4, 64, 128), F32),
            pltpu.VMEM((32, 128), F32),
            pltpu.VMEM((BRICK, 16, 16, 128), BF),
            pltpu.VMEM((256, 128), F32),
            pltpu.VMEM((BRICK, 2, 128, 4096), BF),
            pltpu.VMEM((RAY, 48, 128), BF),
            pltpu.VMEM((RAY, 64, 128), BF),
            pltpu.VMEM((64, 128), F32),
            pltpu.VMEM((4, 16, 16, 128), BF),
            pltpu.VMEM((4, 16, 16, 128), BF),
            pltpu.VMEM((4, 16, 16, 128), BF),
            pltpu.VMEM((3, 16, 16, 128), BF),
            pltpu.VMEM((4, 16, 128), BF),
            pltpu.VMEM((4, 16, 128), BF),
            pltpu.VMEM((2, 16, 128), BF),
            pltpu.VMEM((BRICK, 16, 128), BF),
            pltpu.VMEM((2, 4, 8, 128), F32),
            pltpu.VMEM((288, 128), F32),
            pltpu.VMEM((4, 72, 128), F32),
            dma((3,)),
            dma((BRICK,)),
            dma((BRICK,)),
            dma((4,)),
            dma((8,)),
            dma((9,)),
        ],
        compiler_params=pltpu.CompilerParams(
            collective_id=0, has_side_effects=True, vmem_limit_bytes=48 * 1024 * 1024
        ),
    )(*(pltpu.with_memory_space_constraint(array, pltpu.HBM) for array in inputs))
    restored, residual = pl.pallas_call(
        sweeps_kernel,
        out_shape=(
            jax.ShapeDtypeStruct((4, 64, 128), F32),
            jax.ShapeDtypeStruct((32, 128), F32),
        ),
        in_specs=[pl.BlockSpec(memory_space=pltpu.VMEM)] * 2,
        out_specs=(pl.BlockSpec(memory_space=pltpu.HBM),) * 2,
        scratch_shapes=[pltpu.VMEM((4, 64, 128), F32), dma((2,))],
        compiler_params=pltpu.CompilerParams(vmem_limit_bytes=16 * 1024 * 1024),
    )(start, residual)
    return restored, residual.reshape(sinogram.shape)


def solution(mesh):
    return jax.shard_map(
        shards,
        mesh=mesh,
        in_specs=(
            P(None, ("ray", "brick"), None),
            P("brick", "ray", None, None),
            P("brick", "ray"),
            P("brick", "ray", None, None),
        ),
        out_specs=(P(None, ("ray", "brick"), None), P("brick", "ray", None, None)),
        check_vma=False,
    )
```

```python
import jax
import jax.numpy as jnp
from jax import lax
from jax.experimental import pallas as pl
from jax.experimental.pallas import tpu as pltpu
from jax.sharding import PartitionSpec as P

RAY = 16
BRICK = 8
SWEEPS = 3
MESH = pl.DeviceIdType.MESH
BF = jnp.bfloat16
F32 = jnp.float32

step_size = 0.5
tv_step = 0.28
tv_weight = 0.5


def slot_offsets(m):
    third = (m + 2) // 4
    middle, last = third % 2, third // 2
    return (
        middle * (1 + 2 * (m % 2)) + 2 * last,
        middle * (m // 4) + (1 - middle) * (m % 2),
    )


def far_first(g):
    return (2 + g + (g // 2) * (1 - 2 * (g % 2))) % 4


def ring_step(g):
    middle = ((g + 1) // 2) % 2
    return far_first(g), middle * (4 - g) + (1 - middle) * (6 - 2 * g), 1 + middle


def kernel(
    est_hbm, blocks_hbm, bundle_hbm, sino_hbm,
    out_ref, res_ref,
    bundles, est, sino, tiles, tmp, weights, meta, contrib, picked, select_own, stage, mate_out, mate_in, grad_out, grad_in,
    halo_top, halo_low, far_out, far_in, est_edges, gathered, anchor,
    load_sem, weight_sem, tile_recv, mate_recv, send_sem, recv_sem,
):
    ray = lax.axis_index("ray")
    brick = lax.axis_index("brick")
    z, core = brick // 2, brick % 2
    mate = 2 * z + 1 - core
    ray_x, ray_y = ray // 4, ray % 4

    def each(count, body):
        def step(n, _):
            body(n)
            return 0

        lax.fori_loop(0, count, step, 0)

    def ray_step(n):
        dx, dy = far_first(n // 4), far_first(n % 4)
        peer = ((ray_x + dx) % 4) * 4 + (ray_y + dy) % 4
        return peer, ((4 - dx) % 4) * 4 + (4 - dy) % 4

    def tile_row(m):
        dz, dc = slot_offsets(m)
        return ((z + dz) % 4) * 2 + (core + dc) % 2

    def remote(src, dst, send, recv, to_ray, to_brick):
        return pltpu.make_async_remote_copy(
            src_ref=src, dst_ref=dst, send_sem=send, recv_sem=recv,
            device_id={"ray": to_ray, "brick": to_brick}, device_id_type=MESH,
        )

    def wait_bytes(ref, sem):
        pltpu.make_async_copy(ref, ref, sem).wait()

    load_est = pltpu.make_async_copy(est_hbm, est, load_sem.at[0])
    load_sino = pltpu.make_async_copy(sino_hbm, sino, load_sem.at[1])
    load_bundle = pltpu.make_async_copy(bundle_hbm, bundles, load_sem.at[2])
    load_est.start()

    barrier = pltpu.get_barrier_semaphore()

    def greet(to_ray, to_brick):
        pl.semaphore_signal(barrier, inc=1, device_id={"ray": to_ray, "brick": to_brick}, device_id_type=MESH)

    each(BRICK - 1, lambda n: greet(ray, (brick + n + 1) % BRICK))
    each(RAY - 1, lambda n: greet(ray_step(n)[0], brick))

    @pl.when(brick == 0)
    def _():
        each(BRICK, lambda b: greet((ray + RAY - 1) % RAY, b))

    @pl.when(brick == BRICK - 1)
    def _():
        each(BRICK, lambda b: greet((ray + 1) % RAY, b))

    load_sino.start()
    load_bundle.start()

    def load_block(m):
        pltpu.make_async_copy(
            blocks_hbm.at[0, pl.ds(2 * tile_row(m), 2)], weights.at[m], weight_sem.at[m]
        ).start()

    each(BRICK, load_block)

    lane = lax.broadcasted_iota(jnp.int32, (8, 128), 1)
    row = lax.broadcasted_iota(jnp.int32, (8, 128), 0)
    lane32 = lax.broadcasted_iota(jnp.int32, (32, 128), 1)

    load_est.wait()

    def lay_out(s):
        even = est[s, pl.ds(0, 32, stride=2), :]
        odd = est[s, pl.ds(1, 32, stride=2), :]
        tmp[pl.ds(s, 32, stride=8), :] = jnp.where(lane32 < 64, even, pltpu.roll(odd, 64, 1))
        tmp[pl.ds(4 + s, 32, stride=8), :] = jnp.where(lane32 < 64, pltpu.roll(even, 64, 1), odd)

    each(4, lay_out)
    tiles[0] = tmp[...].astype(BF).reshape(16, 16, 128)

    pl.semaphore_wait(barrier, BRICK - 1 + RAY - 1 + 2)

    remote(tiles.at[0], tiles.at[1], send_sem.at[0], tile_recv.at[1], ray, mate).start()
    for step, slot in ((1, 2), (3, 3), (2, 6)):
        to = ((z + 4 - step) % 4) * 2 + core
        remote(tiles.at[0], tiles.at[slot], send_sem.at[0], tile_recv.at[slot], ray, to).start()

    load_bundle.wait()
    row_keys = []
    lane_key = jnp.zeros((8, 128), F32)
    for m in range(BRICK):
        first = bundles[0, 2 * tile_row(m)].astype(F32)
        second = bundles[0, 2 * tile_row(m) + 1].astype(F32)
        both = jnp.where(row < 4, first, second)
        row_keys.append(both * 4.0 + (row % 4).astype(F32))
        lane_key = jnp.where((lane % 64) // 8 == m, jnp.where((lane // 4) % 2 == 0, first, second), lane_key)
    load_sino.wait()
    meta[0, 0:32, :] = sino[...].astype(BF)
    meta[0, 32:48, :] = jnp.concatenate([lane_key, lane_key], axis=0).astype(BF)

    def send_meta(n):
        peer, slot = ray_step(n)
        remote(meta.at[0], meta.at[slot], send_sem.at[1], recv_sem.at[1], peer, brick).start()

    each(RAY - 1, send_meta)

    above = (brick + BRICK - 1) % BRICK
    above_ray = (ray + (brick + BRICK - 1) // BRICK + RAY - 1) % RAY
    below = (brick + 1) % BRICK
    below_ray = (ray + (brick + 1) // BRICK) % RAY
    remote(
        est.at[:, pl.ds(56, 8), :], est_edges.at[0], send_sem.at[2], recv_sem.at[2], below_ray, below
    ).start()
    remote(
        est.at[:, pl.ds(0, 8), :], est_edges.at[1], send_sem.at[2], recv_sem.at[2], above_ray, above
    ).start()

    def project(m):
        @pl.when(m > 0)
        def _():
            wait_bytes(tiles.at[m], tile_recv.at[m])

        @pl.when((m == 2) | (m == 3) | (m == 6))
        def _():
            slot = m + 2 - m // 6
            remote(tiles.at[m], tiles.at[slot], send_sem.at[0], tile_recv.at[slot], ray, mate).start()

        wait_bytes(weights.at[m], weight_sem.at[m])

        def add_columns(n, full):
            held = tiles[m, pl.ds(4 * n, 4)].astype(F32)
            left = jnp.concatenate(
                [half for c in range(4) for half in (held[c, 0:8], held[c, 8:16])], axis=1
            ).astype(BF)
            columns = pl.ds(pl.multiple_of(n * 1024, 1024), 1024)
            return full + lax.dot_general(
                left, weights[m, :, :, columns].reshape(256, 1024), (((1,), (1,)), ((), ())),
                preferred_element_type=F32,
            )

        full = lax.fori_loop(0, 4, add_columns, jnp.zeros((8, 256), F32))
        picked[pl.ds(pl.multiple_of(m * 8, 8), 8), :] = jnp.where(row < 4, full[:, :128], full[:, 128:])

        def hand_out(at):
            contrib[0, at, :] = picked[at, :].astype(BF)

            def send(n):
                peer, slot = ray_step(n)
                remote(
                    contrib.at[0, at], contrib.at[slot, at], send_sem.at[3], recv_sem.at[3], peer, brick
                ).start()

            each(RAY - 1, send)

        pl.when(m == 5)(lambda: hand_out(pl.ds(0, 48)))
        pl.when(m == 7)(lambda: hand_out(pl.ds(48, 16)))

    each(BRICK, project)

    wait_bytes(meta.at[pl.ds(1, RAY - 1)], recv_sem.at[1])
    own_first = (ray * 32).astype(F32)
    for b in range(4):
        row_keys.append(own_first + (b * 8 + row).astype(F32))
    row_keys = jnp.concatenate(row_keys, axis=0)
    columns = []
    for q in range(RAY // 2):
        key = jnp.where(
            lane < 64, meta[2 * q, 32:48, :].astype(F32)[0:8], meta[2 * q + 1, 32:48, :].astype(F32)[0:8]
        ) * 4.0 + (lane % 4).astype(F32)
        columns.append(jnp.where(row_keys == jnp.concatenate([key] * 12, axis=0), 1.0, 0.0))
    select = jnp.concatenate(columns, axis=1).astype(BF)
    sino_columns = []
    for q in range(4):
        owner = ((ray_x + q) % 4) * 4 + (ray_y + lane // 32) % 4
        key = (owner * 32 + lane % 32).astype(F32)
        sino_columns.append(jnp.where(row_keys[0:64] == jnp.concatenate([key] * 8, axis=0), 1.0, 0.0))
    sino_picked = jnp.dot(
        jnp.concatenate(sino_columns, axis=1).astype(BF), meta[:, 0:32, :].reshape(512, 128),
        preferred_element_type=F32,
    )
    select_own[...] = select[64:96]

    wait_bytes(contrib.at[pl.ds(1, RAY - 1)], recv_sem.at[3])
    picked[...] = (
        jnp.dot(select[0:64], contrib[...].reshape(1024, 128), preferred_element_type=F32) - sino_picked
    )

    def split_left(m):
        mine = picked[pl.ds(pl.multiple_of(m * 8, 8), 8), :]
        return jnp.concatenate(
            [jnp.where(row < 4, mine, 0.0), jnp.where(row < 4, 0.0, mine)], axis=1
        ).astype(BF)

    for edge, (last, column) in enumerate(((BRICK - 1, 15), (0, 0))):
        dz = (last // 2 + 4 - z) % 4
        dc = (last + core) % 2
        odd = dz % 2
        m = odd * (2 + dz // 2 + 2 * dc) + (1 - odd) * (3 * dz + dc)
        rim = jnp.dot(
            split_left(m),
            weights[m, :, :, column * 256 : column * 256 + 256].reshape(256, 256),
            preferred_element_type=F32,
        )
        far_out[edge] = jnp.concatenate([rim[:, :128], rim[:, 128:]], axis=0).astype(BF)
        remote(
            far_out.at[edge], far_in.at[brick], send_sem.at[7], recv_sem.at[7],
            (ray + (1, RAY - 1)[edge]) % RAY, (0, BRICK - 1)[edge],
        ).start()

    def backproject(t):
        pass_on = (t == 0) | ((t % 2 == 1) & (t < 7))
        g = jnp.where(pass_on, t + 1, t - 1) // 2
        dz, first, stride = ring_step(g)
        dc = jnp.where(pass_on, 1, 0)
        m = first + dc * stride
        left = split_left(m)

        def fill(n):
            columns = pl.ds(pl.multiple_of(n * 1024, 1024), 1024)
            spread = jnp.dot(
                left, weights[m, :, :, columns].reshape(256, 1024), preferred_element_type=F32
            )
            for c in range(4):
                stage[4 * n + c, 0:8] = spread[:, c * 256 : c * 256 + 128]
                stage[4 * n + c, 8:16] = spread[:, c * 256 + 128 : c * 256 + 256]

        each(4, fill)

        @pl.when(pass_on)
        def _():
            mate_out[g] = stage[...].astype(BF)
            remote(mate_out.at[g], mate_in.at[g], send_sem.at[4], mate_recv.at[g], ray, mate).start()

        @pl.when(jnp.logical_not(pass_on))
        def _():
            wait_bytes(mate_in.at[g], mate_recv.at[g])
            grad_out[g] = (stage[...] + mate_in[g].astype(F32)).astype(BF)
            target = ((z + dz) % 4) * 2 + core

            @pl.when(g < 3)
            def _():
                remote(grad_out.at[g], grad_in.at[g], send_sem.at[5], recv_sem.at[5], ray, target).start()

            @pl.when(target < BRICK - 1)
            def _():
                remote(
                    grad_out.at[g, 15], halo_top.at[z], send_sem.at[6], recv_sem.at[6], ray, target + 1
                ).start()

            @pl.when(target > 0)
            def _():
                remote(
                    grad_out.at[g, 0], halo_low.at[z], send_sem.at[6], recv_sem.at[8], ray, target - 1
                ).start()

    each(BRICK, backproject)

    res_ref[...] = (
        jnp.dot(select_own[...], contrib[...].reshape(1024, 128), preferred_element_type=F32) - sino[...]
    )

    wait_bytes(est_edges, recv_sem.at[2])
    wait_bytes(grad_in, recv_sem.at[5])
    total = grad_out[3].astype(F32)
    for g in range(3):
        total += grad_in[g].astype(F32)
    gathered[16:272, :] = total.reshape(256, 128)

    @pl.when(brick > 0)
    def _():
        wait_bytes(halo_top, recv_sem.at[6])
        gathered[0:16, :] = halo_top[...].astype(F32).sum(axis=0)

    @pl.when(brick < BRICK - 1)
    def _():
        wait_bytes(halo_low, recv_sem.at[8])
        gathered[272:288, :] = halo_low[...].astype(F32).sum(axis=0)

    @pl.when(brick == 0)
    def _():
        wait_bytes(far_in, recv_sem.at[7])
        gathered[0:16, :] = far_in[...].astype(F32).sum(axis=0)

    @pl.when(brick == BRICK - 1)
    def _():
        wait_bytes(far_in, recv_sem.at[7])
        gathered[272:288, :] = far_in[...].astype(F32).sum(axis=0)

    lane36 = lax.broadcasted_iota(jnp.int32, (36, 128), 1)

    def put_back(s):
        one = gathered[pl.ds(s, 36, stride=8), :]
        two = gathered[pl.ds(4 + s, 36, stride=8), :]
        anchor[s, pl.ds(0, 36, stride=2), :] = jnp.where(lane36 < 64, one, pltpu.roll(two, 64, 1))
        anchor[s, pl.ds(1, 36, stride=2), :] = jnp.where(lane36 < 64, pltpu.roll(one, 64, 1), two)

    each(4, put_back)
    image = jnp.concatenate([est_edges[0, :, 4:8, :], est[...], est_edges[1, :, 0:4, :]], axis=1)
    start = image - step_size * anchor[...]

    out_ref[...] = start

    wait_bytes(tiles.at[pl.ds(1, BRICK - 1)], send_sem.at[0])
    wait_bytes(meta.at[pl.ds(1, RAY - 1)], send_sem.at[1])
    wait_bytes(est_edges, send_sem.at[2])
    wait_bytes(contrib.at[pl.ds(1, RAY - 1)], send_sem.at[3])
    wait_bytes(mate_in, send_sem.at[4])
    wait_bytes(grad_in, send_sem.at[5])
    wait_bytes(tiles.at[0, pl.ds(0, 7)], send_sem.at[6])
    wait_bytes(far_out, send_sem.at[7])


def sweeps_kernel(start_ref, res_ref, out_hbm, res_hbm, out, primal, extra, dual_y, dual_x, dual_z, save_sem):
    ray = lax.axis_index("ray")
    brick = lax.axis_index("brick")
    save_res = pltpu.make_async_copy(res_ref, res_hbm, save_sem.at[0])
    save_out = pltpu.make_async_copy(out, out_hbm, save_sem.at[1])
    save_res.start()

    shape = (4, 72, 128)
    rows = lax.broadcasted_iota(jnp.int32, shape, 1)
    lanes = lax.broadcasted_iota(jnp.int32, shape, 2)
    at_start = (ray == 0) & (brick == 0)
    at_end = (ray == RAY - 1) & (brick == BRICK - 1)
    above_image = (rows < 4) & at_start
    below_image = (rows >= 68) & at_end
    last_lane = lanes == 127
    first_lane = lanes == 0
    level = jnp.zeros((1, 72, 128), F32)

    start = jnp.where(below_image, 0.0, start_ref[...])
    primal[...] = start
    extra[...] = start
    for dual in (dual_y, dual_x, dual_z):
        dual[...] = jnp.zeros(shape, F32)

    def sweep(n, _):
        ahead = extra[...]
        diff_y = pltpu.roll(ahead, 71, 1) - ahead
        diff_x = jnp.where(last_lane, 0.0, pltpu.roll(ahead, 127, 2)) - ahead
        diff_z = jnp.concatenate([ahead[1:] - ahead[:-1], level], axis=0)
        trial_y = dual_y[...] + tv_step * diff_y
        trial_x = dual_x[...] + tv_step * diff_x
        trial_z = dual_z[...] + tv_step * diff_z
        norm = trial_y * trial_y + trial_x * trial_x + trial_z * trial_z
        shrink = lax.rsqrt(jnp.maximum(1.0, norm * (1.0 / (tv_weight * tv_weight))))
        new_y = jnp.where(above_image, 0.0, trial_y * shrink)
        new_x = trial_x * shrink
        new_z = trial_z * shrink
        dual_y[...] = new_y
        dual_x[...] = new_x
        dual_z[...] = new_z
        div = new_y - pltpu.roll(new_y, 1, 1)
        div += new_x - jnp.where(first_lane, 0.0, pltpu.roll(new_x, 1, 2))
        div += new_z - jnp.concatenate([level, new_z[:-1]], axis=0)
        before = primal[...]
        updated = (before + tv_step * div + tv_step * start_ref[...]) * (1.0 / (1.0 + tv_step))
        extra[...] = jnp.where(below_image, 0.0, 2.0 * updated - before)
        primal[...] = updated
        return 0

    lax.fori_loop(0, SWEEPS, sweep, 0)
    out[...] = primal[:, 4:68, :]
    save_out.start()
    save_res.wait()
    save_out.wait()


def shards(estimate, blocks, block_bundle, sinogram):
    dma = pltpu.SemaphoreType.DMA
    inputs = (estimate, blocks, block_bundle, sinogram.reshape(32, 128))
    start, residual = pl.pallas_call(
        kernel,
        out_shape=(
            jax.ShapeDtypeStruct((4, 72, 128), F32),
            jax.ShapeDtypeStruct((32, 128), F32),
        ),
        in_specs=[pl.BlockSpec(memory_space=pltpu.HBM)] * 4,
        out_specs=(pl.BlockSpec(memory_space=pltpu.VMEM), pl.BlockSpec(memory_space=pltpu.VMEM)),
        scratch_shapes=[
            pltpu.SMEM((1, 16), jnp.int32),
            pltpu.VMEM((4, 64, 128), F32),
            pltpu.VMEM((32, 128), F32),
            pltpu.VMEM((BRICK, 16, 16, 128), BF),
            pltpu.VMEM((256, 128), F32),
            pltpu.VMEM((BRICK, 2, 128, 4096), BF),
            pltpu.VMEM((RAY, 48, 128), BF),
            pltpu.VMEM((RAY, 64, 128), BF),
            pltpu.VMEM((64, 128), F32),
            pltpu.VMEM((32, 1024), BF),
            pltpu.VMEM((16, 16, 128), F32),
            pltpu.VMEM((4, 16, 16, 128), BF),
            pltpu.VMEM((4, 16, 16, 128), BF),
            pltpu.VMEM((4, 16, 16, 128), BF),
            pltpu.VMEM((3, 16, 16, 128), BF),
            pltpu.VMEM((4, 16, 128), BF),
            pltpu.VMEM((4, 16, 128), BF),
            pltpu.VMEM((2, 16, 128), BF),
            pltpu.VMEM((BRICK, 16, 128), BF),
            pltpu.VMEM((2, 4, 8, 128), F32),
            pltpu.VMEM((288, 128), F32),
            pltpu.VMEM((4, 72, 128), F32),
            dma((3,)),
            dma((BRICK,)),
            dma((BRICK,)),
            dma((4,)),
            dma((8,)),
            dma((9,)),
        ],
        compiler_params=pltpu.CompilerParams(
            collective_id=0, has_side_effects=True, vmem_limit_bytes=48 * 1024 * 1024
        ),
    )(*(pltpu.with_memory_space_constraint(array, pltpu.HBM) for array in inputs))
    restored, residual = pl.pallas_call(
        sweeps_kernel,
        out_shape=(
            jax.ShapeDtypeStruct((4, 64, 128), F32),
            jax.ShapeDtypeStruct((32, 128), F32),
        ),
        in_specs=[pl.BlockSpec(memory_space=pltpu.VMEM)] * 2,
        out_specs=(pl.BlockSpec(memory_space=pltpu.HBM),) * 2,
        scratch_shapes=[pltpu.VMEM((4, 64, 128), F32)] + [pltpu.VMEM((4, 72, 128), F32)] * 5 + [dma((2,))],
        compiler_params=pltpu.CompilerParams(vmem_limit_bytes=16 * 1024 * 1024),
    )(start, residual)
    return restored, residual.reshape(sinogram.shape)


def solution(mesh):
    return jax.shard_map(
        shards,
        mesh=mesh,
        in_specs=(
            P(None, ("ray", "brick"), None),
            P("brick", "ray", None, None),
            P("brick", "ray"),
            P("brick", "ray", None, None),
        ),
        out_specs=(P(None, ("ray", "brick"), None), P("brick", "ray", None, None)),
        check_vma=False,
    )
```

```python
import jax
import jax.numpy as jnp
from jax import lax
from jax.experimental import pallas as pl
from jax.experimental.pallas import tpu as pltpu
from jax.sharding import PartitionSpec as P

RAY = 16
BRICK = 8
SWEEPS = 3
MESH = pl.DeviceIdType.MESH
BF = jnp.bfloat16
F32 = jnp.float32

step_size = 0.5
tv_step = 0.28
tv_weight = 0.5


def slot_offsets(m):
    third = (m + 2) // 4
    middle, last = third % 2, third // 2
    return (
        middle * (1 + 2 * (m % 2)) + 2 * last,
        middle * (m // 4) + (1 - middle) * (m % 2),
    )


RAY_STEPS = sorted(
    ((dx, dy) for dx in range(4) for dy in range(4) if dx or dy),
    key=lambda step: -(min(step[0], 4 - step[0]) + min(step[1], 4 - step[1])),
)


def ring_step(g):
    middle = ((g + 1) // 2) % 2
    step = (2 + g + (g // 2) * (1 - 2 * (g % 2))) % 4
    return step, middle * (4 - g) + (1 - middle) * (6 - 2 * g), 1 + middle


def kernel(
    est_hbm, blocks_hbm, bundle_hbm, sino_hbm,
    out_ref, res_ref,
    bundles, est, sino, tiles, tmp, weights, meta, contrib, picked, select_own, mate_out, mate_in, grad_out, grad_in,
    halo_top, halo_low, far_out, far_in, est_edges, gathered, anchor,
    load_sem, weight_sem, tile_recv, mate_recv, send_sem, recv_sem,
):
    ray = lax.axis_index("ray")
    brick = lax.axis_index("brick")
    z, core = brick // 2, brick % 2
    mate = 2 * z + 1 - core
    ray_x, ray_y = ray // 4, ray % 4

    def ray_peer(dx, dy):
        return ((ray_x + dx) % 4) * 4 + (ray_y + dy) % 4

    def ray_slot(dx, dy):
        return ((4 - dx) % 4) * 4 + (4 - dy) % 4

    def tile_row(m):
        dz, dc = slot_offsets(m)
        return ((z + dz) % 4) * 2 + (core + dc) % 2

    def remote(src, dst, send, recv, to_ray, to_brick):
        return pltpu.make_async_remote_copy(
            src_ref=src, dst_ref=dst, send_sem=send, recv_sem=recv,
            device_id={"ray": to_ray, "brick": to_brick}, device_id_type=MESH,
        )

    def wait_bytes(ref, sem):
        pltpu.make_async_copy(ref, ref, sem).wait()

    load_est = pltpu.make_async_copy(est_hbm, est, load_sem.at[0])
    load_sino = pltpu.make_async_copy(sino_hbm, sino, load_sem.at[1])
    load_bundle = pltpu.make_async_copy(bundle_hbm, bundles, load_sem.at[2])
    load_est.start()

    barrier = pltpu.get_barrier_semaphore()

    def greet(to_ray, to_brick):
        pl.semaphore_signal(barrier, inc=1, device_id={"ray": to_ray, "brick": to_brick}, device_id_type=MESH)

    for m in range(1, BRICK):
        greet(ray, (brick + m) % BRICK)
    for dx, dy in RAY_STEPS:
        greet(ray_peer(dx, dy), brick)

    @pl.when(brick == 0)
    def _():
        for b in range(BRICK):
            greet((ray + RAY - 1) % RAY, b)

    @pl.when(brick == BRICK - 1)
    def _():
        for b in range(BRICK):
            greet((ray + 1) % RAY, b)

    load_sino.start()
    load_bundle.start()

    def load_block(m, _):
        pltpu.make_async_copy(
            blocks_hbm.at[0, pl.ds(2 * tile_row(m), 2)], weights.at[m], weight_sem.at[m]
        ).start()
        return 0

    lax.fori_loop(0, BRICK, load_block, 0)

    lane = lax.broadcasted_iota(jnp.int32, (8, 128), 1)
    row = lax.broadcasted_iota(jnp.int32, (8, 128), 0)
    lane32 = lax.broadcasted_iota(jnp.int32, (32, 128), 1)

    load_est.wait()
    for s in range(4):
        even = est[s, pl.ds(0, 32, stride=2), :]
        odd = est[s, pl.ds(1, 32, stride=2), :]
        tmp[pl.ds(s, 32, stride=8), :] = jnp.where(lane32 < 64, even, pltpu.roll(odd, 64, 1))
        tmp[pl.ds(4 + s, 32, stride=8), :] = jnp.where(lane32 < 64, pltpu.roll(even, 64, 1), odd)
    tiles[0] = tmp[...].astype(BF).reshape(16, 16, 128)

    pl.semaphore_wait(barrier, BRICK - 1 + RAY - 1 + 2)

    remote(tiles.at[0], tiles.at[1], send_sem.at[0], tile_recv.at[1], ray, mate).start()
    for step, slot in ((1, 2), (3, 3), (2, 6)):
        to = ((z + 4 - step) % 4) * 2 + core
        remote(tiles.at[0], tiles.at[slot], send_sem.at[0], tile_recv.at[slot], ray, to).start()

    load_bundle.wait()
    row_keys = []
    lane_key = jnp.zeros((8, 128), F32)
    for m in range(BRICK):
        first = bundles[0, 2 * tile_row(m)].astype(F32)
        second = bundles[0, 2 * tile_row(m) + 1].astype(F32)
        both = jnp.where(row < 4, first, second)
        row_keys.append(both * 4.0 + (row % 4).astype(F32))
        lane_key = jnp.where((lane % 64) // 8 == m, jnp.where((lane // 4) % 2 == 0, first, second), lane_key)
    load_sino.wait()
    meta[0, 0:32, :] = sino[...].astype(BF)
    meta[0, 32:48, :] = jnp.concatenate([lane_key, lane_key], axis=0).astype(BF)
    for dx, dy in RAY_STEPS:
        remote(
            meta.at[0], meta.at[ray_slot(dx, dy)], send_sem.at[1], recv_sem.at[1], ray_peer(dx, dy), brick
        ).start()

    above = (brick + BRICK - 1) % BRICK
    above_ray = (ray + (brick + BRICK - 1) // BRICK + RAY - 1) % RAY
    below = (brick + 1) % BRICK
    below_ray = (ray + (brick + 1) // BRICK) % RAY
    remote(
        est.at[:, pl.ds(56, 8), :], est_edges.at[0], send_sem.at[2], recv_sem.at[2], below_ray, below
    ).start()
    remote(
        est.at[:, pl.ds(0, 8), :], est_edges.at[1], send_sem.at[2], recv_sem.at[2], above_ray, above
    ).start()

    def project(m, _):
        @pl.when(m > 0)
        def _():
            wait_bytes(tiles.at[m], tile_recv.at[m])

        @pl.when((m == 2) | (m == 3) | (m == 6))
        def _():
            slot = m + 2 - m // 6
            remote(tiles.at[m], tiles.at[slot], send_sem.at[0], tile_recv.at[slot], ray, mate).start()

        wait_bytes(weights.at[m], weight_sem.at[m])
        held = tiles[m].astype(F32)
        left = jnp.concatenate(
            [half for c in range(16) for half in (held[c, 0:8], held[c, 8:16])], axis=1
        ).astype(BF)
        full = lax.dot_general(
            left, weights[m].reshape(256, 4096), (((1,), (1,)), ((), ())), preferred_element_type=F32
        )
        picked[pl.ds(pl.multiple_of(m * 8, 8), 8), :] = jnp.where(row < 4, full[:, :128], full[:, 128:])

        def hand_out(at):
            contrib[0, at, :] = picked[at, :].astype(BF)
            for dx, dy in RAY_STEPS:
                remote(
                    contrib.at[0, at], contrib.at[ray_slot(dx, dy), at], send_sem.at[3], recv_sem.at[3],
                    ray_peer(dx, dy), brick,
                ).start()

        pl.when(m == 5)(lambda: hand_out(pl.ds(0, 48)))
        pl.when(m == 7)(lambda: hand_out(pl.ds(48, 16)))
        return 0

    lax.fori_loop(0, BRICK, project, 0)

    wait_bytes(meta.at[pl.ds(1, RAY - 1)], recv_sem.at[1])
    own_first = (ray * 32).astype(F32)
    for b in range(4):
        row_keys.append(own_first + (b * 8 + row).astype(F32))
    row_keys = jnp.concatenate(row_keys, axis=0)
    columns = []
    for q in range(RAY // 2):
        key = jnp.where(
            lane < 64, meta[2 * q, 32:48, :].astype(F32)[0:8], meta[2 * q + 1, 32:48, :].astype(F32)[0:8]
        ) * 4.0 + (lane % 4).astype(F32)
        columns.append(jnp.where(row_keys == jnp.concatenate([key] * 12, axis=0), 1.0, 0.0))
    select = jnp.concatenate(columns, axis=1).astype(BF)
    sino_columns = []
    for q in range(4):
        owner = ((ray_x + q) % 4) * 4 + (ray_y + lane // 32) % 4
        key = (owner * 32 + lane % 32).astype(F32)
        sino_columns.append(jnp.where(row_keys[0:64] == jnp.concatenate([key] * 8, axis=0), 1.0, 0.0))
    sino_picked = jnp.dot(
        jnp.concatenate(sino_columns, axis=1).astype(BF), meta[:, 0:32, :].reshape(512, 128),
        preferred_element_type=F32,
    )
    select_own[...] = select[64:96]

    wait_bytes(contrib.at[pl.ds(1, RAY - 1)], recv_sem.at[3])
    picked[...] = (
        jnp.dot(select[0:64], contrib[...].reshape(1024, 128), preferred_element_type=F32) - sino_picked
    )

    def split_left(m):
        mine = picked[pl.ds(pl.multiple_of(m * 8, 8), 8), :]
        return jnp.concatenate(
            [jnp.where(row < 4, mine, 0.0), jnp.where(row < 4, 0.0, mine)], axis=1
        ).astype(BF)

    def send_far():
        for edge, (last, column) in enumerate(((BRICK - 1, 15), (0, 0))):
            dz = (last // 2 + 4 - z) % 4
            dc = (last + core) % 2
            odd = dz % 2
            m = odd * (2 + dz // 2 + 2 * dc) + (1 - odd) * (3 * dz + dc)
            rim = jnp.dot(
                split_left(m),
                weights[m, :, :, column * 256 : column * 256 + 256].reshape(256, 256),
                preferred_element_type=F32,
            )
            far_out[edge] = jnp.concatenate([rim[:, :128], rim[:, 128:]], axis=0).astype(BF)
            remote(
                far_out.at[edge], far_in.at[brick], send_sem.at[7], recv_sem.at[7],
                (ray + (1, RAY - 1)[edge]) % RAY, (0, BRICK - 1)[edge],
            ).start()

    def backproject(t, _):
        pass_on = (t == 0) | (t == 1) | (t == 3) | (t == 6)
        g = jnp.where(pass_on, (t + 1) // 2, jnp.where(t == 5, 2, (t - 1) // 2))
        dz, first, stride = ring_step(g)
        dc = jnp.where(pass_on, 1, 0)
        m = first + dc * stride
        spread = jnp.dot(split_left(m), weights[m].reshape(256, 4096), preferred_element_type=F32)
        pieces = [
            jnp.concatenate(
                [spread[:, c * 256 : c * 256 + 128], spread[:, c * 256 + 128 : c * 256 + 256]], axis=0
            )
            for c in range(16)
        ]

        @pl.when(pass_on)
        def _():
            for c in range(16):
                mate_out[g, c] = pieces[c].astype(BF)
            remote(mate_out.at[g], mate_in.at[g], send_sem.at[4], mate_recv.at[g], ray, mate).start()
            pl.when(t == 1)(send_far)

        @pl.when(jnp.logical_not(pass_on))
        def _():
            wait_bytes(mate_in.at[g], mate_recv.at[g])
            for c in range(16):
                grad_out[g, c] = (pieces[c] + mate_in[g, c].astype(F32)).astype(BF)
            target = ((z + dz) % 4) * 2 + core

            @pl.when(g < 3)
            def _():
                remote(grad_out.at[g], grad_in.at[g], send_sem.at[5], recv_sem.at[5], ray, target).start()

            @pl.when(target < BRICK - 1)
            def _():
                remote(
                    grad_out.at[g, 15], halo_top.at[z], send_sem.at[6], recv_sem.at[6], ray, target + 1
                ).start()

            @pl.when(target > 0)
            def _():
                remote(
                    grad_out.at[g, 0], halo_low.at[z], send_sem.at[6], recv_sem.at[8], ray, target - 1
                ).start()

        return 0

    lax.fori_loop(0, BRICK, backproject, 0)

    res_ref[...] = (
        jnp.dot(select_own[...], contrib[...].reshape(1024, 128), preferred_element_type=F32) - sino[...]
    )

    wait_bytes(est_edges, recv_sem.at[2])
    wait_bytes(grad_in, recv_sem.at[5])
    total = grad_out[3].astype(F32)
    for g in range(3):
        total += grad_in[g].astype(F32)
    gathered[16:272, :] = total.reshape(256, 128)

    @pl.when(brick > 0)
    def _():
        wait_bytes(halo_top, recv_sem.at[6])
        gathered[0:16, :] = halo_top[...].astype(F32).sum(axis=0)

    @pl.when(brick < BRICK - 1)
    def _():
        wait_bytes(halo_low, recv_sem.at[8])
        gathered[272:288, :] = halo_low[...].astype(F32).sum(axis=0)

    @pl.when(brick == 0)
    def _():
        wait_bytes(far_in, recv_sem.at[7])
        gathered[0:16, :] = far_in[...].astype(F32).sum(axis=0)

    @pl.when(brick == BRICK - 1)
    def _():
        wait_bytes(far_in, recv_sem.at[7])
        gathered[272:288, :] = far_in[...].astype(F32).sum(axis=0)

    lane36 = lax.broadcasted_iota(jnp.int32, (36, 128), 1)
    for s in range(4):
        one = gathered[pl.ds(s, 36, stride=8), :]
        two = gathered[pl.ds(4 + s, 36, stride=8), :]
        anchor[s, pl.ds(0, 36, stride=2), :] = jnp.where(lane36 < 64, one, pltpu.roll(two, 64, 1))
        anchor[s, pl.ds(1, 36, stride=2), :] = jnp.where(lane36 < 64, pltpu.roll(one, 64, 1), two)
    image = jnp.concatenate([est_edges[0, :, 4:8, :], est[...], est_edges[1, :, 0:4, :]], axis=1)
    start = image - step_size * anchor[...]

    out_ref[...] = start

    wait_bytes(tiles.at[pl.ds(1, BRICK - 1)], send_sem.at[0])
    wait_bytes(meta.at[pl.ds(1, RAY - 1)], send_sem.at[1])
    wait_bytes(est_edges, send_sem.at[2])
    wait_bytes(contrib.at[pl.ds(1, RAY - 1)], send_sem.at[3])
    wait_bytes(mate_in, send_sem.at[4])
    wait_bytes(grad_in, send_sem.at[5])
    wait_bytes(tiles.at[0, pl.ds(0, 7)], send_sem.at[6])
    wait_bytes(far_out, send_sem.at[7])


def sweeps_kernel(start_ref, res_ref, out_hbm, res_hbm, out, save_sem):
    ray = lax.axis_index("ray")
    brick = lax.axis_index("brick")
    save_res = pltpu.make_async_copy(res_ref, res_hbm, save_sem.at[0])
    save_out = pltpu.make_async_copy(out, out_hbm, save_sem.at[1])
    save_res.start()

    shape = (4, 72, 128)
    rows = lax.broadcasted_iota(jnp.int32, shape, 1)
    lanes = lax.broadcasted_iota(jnp.int32, shape, 2)
    at_start = (ray == 0) & (brick == 0)
    at_end = (ray == RAY - 1) & (brick == BRICK - 1)
    above_image = (rows < 4) & at_start
    below_image = (rows >= 68) & at_end
    last_lane = lanes == 127
    first_lane = lanes == 0
    level = jnp.zeros((1, 72, 128), F32)

    start = jnp.where(below_image, 0.0, start_ref[...])
    primal = start
    extra = start
    dual_y = dual_x = dual_z = None
    for sweep in range(SWEEPS):
        diff_y = pltpu.roll(extra, 71, 1) - extra
        diff_x = jnp.where(last_lane, 0.0, pltpu.roll(extra, 127, 2)) - extra
        diff_z = jnp.concatenate([extra[1:] - extra[:-1], level], axis=0)
        trial_y, trial_x, trial_z = tv_step * diff_y, tv_step * diff_x, tv_step * diff_z
        if sweep:
            trial_y, trial_x, trial_z = dual_y + trial_y, dual_x + trial_x, dual_z + trial_z
        norm = trial_y * trial_y + trial_x * trial_x + trial_z * trial_z
        shrink = lax.rsqrt(jnp.maximum(1.0, norm * (1.0 / (tv_weight * tv_weight))))
        dual_y = jnp.where(above_image, 0.0, trial_y * shrink)
        dual_x = trial_x * shrink
        dual_z = trial_z * shrink
        div = dual_y - pltpu.roll(dual_y, 1, 1)
        div += dual_x - jnp.where(first_lane, 0.0, pltpu.roll(dual_x, 1, 2))
        div += dual_z - jnp.concatenate([level, dual_z[:-1]], axis=0)
        updated = (primal + tv_step * div + tv_step * start) * (1.0 / (1.0 + tv_step))
        extra = jnp.where(below_image, 0.0, 2.0 * updated - primal)
        primal = updated
    out[...] = primal[:, 4:68, :]
    save_out.start()
    save_res.wait()
    save_out.wait()


def shards(estimate, blocks, block_bundle, sinogram):
    dma = pltpu.SemaphoreType.DMA
    inputs = (estimate, blocks, block_bundle, sinogram.reshape(32, 128))
    start, residual = pl.pallas_call(
        kernel,
        out_shape=(
            jax.ShapeDtypeStruct((4, 72, 128), F32),
            jax.ShapeDtypeStruct((32, 128), F32),
        ),
        in_specs=[pl.BlockSpec(memory_space=pltpu.HBM)] * 4,
        out_specs=(pl.BlockSpec(memory_space=pltpu.VMEM), pl.BlockSpec(memory_space=pltpu.VMEM)),
        scratch_shapes=[
            pltpu.SMEM((1, 16), jnp.int32),
            pltpu.VMEM((4, 64, 128), F32),
            pltpu.VMEM((32, 128), F32),
            pltpu.VMEM((BRICK, 16, 16, 128), BF),
            pltpu.VMEM((256, 128), F32),
            pltpu.VMEM((BRICK, 2, 128, 4096), BF),
            pltpu.VMEM((RAY, 48, 128), BF),
            pltpu.VMEM((RAY, 64, 128), BF),
            pltpu.VMEM((64, 128), F32),
            pltpu.VMEM((32, 1024), BF),
            pltpu.VMEM((4, 16, 16, 128), BF),
            pltpu.VMEM((4, 16, 16, 128), BF),
            pltpu.VMEM((4, 16, 16, 128), BF),
            pltpu.VMEM((3, 16, 16, 128), BF),
            pltpu.VMEM((4, 16, 128), BF),
            pltpu.VMEM((4, 16, 128), BF),
            pltpu.VMEM((2, 16, 128), BF),
            pltpu.VMEM((BRICK, 16, 128), BF),
            pltpu.VMEM((2, 4, 8, 128), F32),
            pltpu.VMEM((288, 128), F32),
            pltpu.VMEM((4, 72, 128), F32),
            dma((3,)),
            dma((BRICK,)),
            dma((BRICK,)),
            dma((4,)),
            dma((8,)),
            dma((9,)),
        ],
        compiler_params=pltpu.CompilerParams(
            collective_id=0, has_side_effects=True, vmem_limit_bytes=48 * 1024 * 1024
        ),
    )(*(pltpu.with_memory_space_constraint(array, pltpu.HBM) for array in inputs))
    restored, residual = pl.pallas_call(
        sweeps_kernel,
        out_shape=(
            jax.ShapeDtypeStruct((4, 64, 128), F32),
            jax.ShapeDtypeStruct((32, 128), F32),
        ),
        in_specs=[pl.BlockSpec(memory_space=pltpu.VMEM)] * 2,
        out_specs=(pl.BlockSpec(memory_space=pltpu.HBM),) * 2,
        scratch_shapes=[pltpu.VMEM((4, 64, 128), F32), dma((2,))],
        compiler_params=pltpu.CompilerParams(vmem_limit_bytes=16 * 1024 * 1024),
    )(start, residual)
    return restored, residual.reshape(sinogram.shape)


def solution(mesh):
    return jax.shard_map(
        shards,
        mesh=mesh,
        in_specs=(
            P(None, ("ray", "brick"), None),
            P("brick", "ray", None, None),
            P("brick", "ray"),
            P("brick", "ray", None, None),
        ),
        out_specs=(P(None, ("ray", "brick"), None), P("brick", "ray", None, None)),
        check_vma=False,
    )
```

```python
import jax
import jax.numpy as jnp
from jax import lax
from jax.experimental import pallas as pl
from jax.experimental.pallas import tpu as pltpu
from jax.sharding import PartitionSpec as P

RAY = 16
BRICK = 8
SWEEPS = 3
MESH = pl.DeviceIdType.MESH
BF = jnp.bfloat16
F32 = jnp.float32

step_size = 0.5
tv_step = 0.28
tv_weight = 0.5


def slot_offsets(m):
    third = (m + 2) // 4
    middle, last = third % 2, third // 2
    return (
        middle * (1 + 2 * (m % 2)) + 2 * last,
        middle * (m // 4) + (1 - middle) * (m % 2),
    )


RAY_STEPS = sorted(
    ((dx, dy) for dx in range(4) for dy in range(4) if dx or dy),
    key=lambda step: -(min(step[0], 4 - step[0]) + min(step[1], 4 - step[1])),
)


def ring_step(g):
    middle = ((g + 1) // 2) % 2
    step = (2 + g + (g // 2) * (1 - 2 * (g % 2))) % 4
    return step, middle * (4 - g) + (1 - middle) * (6 - 2 * g), 1 + middle


def kernel(
    est_hbm, blocks_hbm, bundle_hbm, sino_hbm,
    out_ref, res_ref,
    bundles, est, sino, tiles, tmp, weights, meta, contrib, picked, select_own, mate_out, mate_in, grad_out, grad_in,
    halo_top, halo_low, far_out, far_in, est_edges, gathered, anchor,
    line_sem, load_sem, weight_sem, tile_recv, mate_recv, send_sem, recv_sem,
):
    ray = lax.axis_index("ray")
    brick = lax.axis_index("brick")
    z, core = brick // 2, brick % 2
    mate = 2 * z + 1 - core
    ray_x, ray_y = ray // 4, ray % 4

    def ray_peer(dx, dy):
        return ((ray_x + dx) % 4) * 4 + (ray_y + dy) % 4

    def ray_slot(dx, dy):
        return ((4 - dx) % 4) * 4 + (4 - dy) % 4

    def tile_row(m):
        dz, dc = slot_offsets(m)
        return ((z + dz) % 4) * 2 + (core + dc) % 2

    def remote(src, dst, send, recv, to_ray, to_brick):
        return pltpu.make_async_remote_copy(
            src_ref=src, dst_ref=dst, send_sem=send, recv_sem=recv,
            device_id={"ray": to_ray, "brick": to_brick}, device_id_type=MESH,
        )

    def wait_bytes(ref, sem):
        pltpu.make_async_copy(ref, ref, sem).wait()

    load_est = pltpu.make_async_copy(est_hbm, est, load_sem.at[0])
    load_sino = pltpu.make_async_copy(sino_hbm, sino, load_sem.at[1])
    load_bundle = pltpu.make_async_copy(bundle_hbm, bundles, load_sem.at[2])
    load_est.start()

    barrier = pltpu.get_barrier_semaphore()

    def greet(to_ray, to_brick):
        pl.semaphore_signal(barrier, inc=1, device_id={"ray": to_ray, "brick": to_brick}, device_id_type=MESH)

    for m in range(1, BRICK):
        greet(ray, (brick + m) % BRICK)
    for d in range(1, 4):
        greet(ray_peer(d, 0), brick)
        greet(ray_peer(0, d), brick)

    load_sino.start()
    load_bundle.start()

    def load_block(m, _):
        pltpu.make_async_copy(
            blocks_hbm.at[0, pl.ds(2 * tile_row(m), 2)], weights.at[m], weight_sem.at[m]
        ).start()
        return 0

    lax.fori_loop(0, BRICK, load_block, 0)

    lane = lax.broadcasted_iota(jnp.int32, (8, 128), 1)
    row = lax.broadcasted_iota(jnp.int32, (8, 128), 0)
    lane32 = lax.broadcasted_iota(jnp.int32, (32, 128), 1)

    load_est.wait()
    for s in range(4):
        even = est[s, pl.ds(0, 32, stride=2), :]
        odd = est[s, pl.ds(1, 32, stride=2), :]
        tmp[pl.ds(s, 32, stride=8), :] = jnp.where(lane32 < 64, even, pltpu.roll(odd, 64, 1))
        tmp[pl.ds(4 + s, 32, stride=8), :] = jnp.where(lane32 < 64, pltpu.roll(even, 64, 1), odd)
    tiles[0] = tmp[...].astype(BF).reshape(16, 16, 128)

    pl.semaphore_wait(barrier, BRICK - 1 + 6)

    remote(tiles.at[0], tiles.at[1], send_sem.at[0], tile_recv.at[1], ray, mate).start()
    for step, slot in ((1, 2), (3, 3), (2, 6)):
        to = ((z + 4 - step) % 4) * 2 + core
        remote(tiles.at[0], tiles.at[slot], send_sem.at[0], tile_recv.at[slot], ray, to).start()

    for d in range(1, 4):
        pl.semaphore_signal(
            line_sem, inc=1, device_id={"ray": ray_peer(d, 0), "brick": brick}, device_id_type=MESH
        )

    load_bundle.wait()
    row_keys = []
    lane_key = jnp.zeros((8, 128), F32)
    for m in range(BRICK):
        first = bundles[0, 2 * tile_row(m)].astype(F32)
        second = bundles[0, 2 * tile_row(m) + 1].astype(F32)
        both = jnp.where(row < 4, first, second)
        row_keys.append(both * 4.0 + (row % 4).astype(F32))
        lane_key = jnp.where((lane % 64) // 8 == m, jnp.where((lane // 4) % 2 == 0, first, second), lane_key)
    load_sino.wait()
    meta[0, 0:32, :] = sino[...].astype(BF)
    meta[0, 32:48, :] = jnp.concatenate([lane_key, lane_key], axis=0).astype(BF)
    def send_meta():
        pl.semaphore_wait(line_sem, 3)
        for dx, dy in RAY_STEPS:
            remote(
                meta.at[0], meta.at[ray_slot(dx, dy)], send_sem.at[1], recv_sem.at[1], ray_peer(dx, dy), brick
            ).start()

    def project(m, _):
        @pl.when(m > 0)
        def _():
            wait_bytes(tiles.at[m], tile_recv.at[m])

        @pl.when((m == 2) | (m == 3) | (m == 6))
        def _():
            slot = m + 2 - m // 6
            remote(tiles.at[m], tiles.at[slot], send_sem.at[0], tile_recv.at[slot], ray, mate).start()

        wait_bytes(weights.at[m], weight_sem.at[m])
        held = tiles[m].astype(F32)
        left = jnp.concatenate(
            [half for c in range(16) for half in (held[c, 0:8], held[c, 8:16])], axis=1
        ).astype(BF)
        full = lax.dot_general(
            left, weights[m].reshape(256, 4096), (((1,), (1,)), ((), ())), preferred_element_type=F32
        )
        picked[pl.ds(pl.multiple_of(m * 8, 8), 8), :] = jnp.where(row < 4, full[:, :128], full[:, 128:])

        def hand_out(at):
            contrib[0, at, :] = picked[at, :].astype(BF)
            for dx, dy in RAY_STEPS:
                remote(
                    contrib.at[0, at], contrib.at[ray_slot(dx, dy), at], send_sem.at[3], recv_sem.at[3],
                    ray_peer(dx, dy), brick,
                ).start()

        pl.when(m == 1)(send_meta)
        pl.when(m == 5)(lambda: hand_out(pl.ds(0, 48)))
        pl.when(m == 7)(lambda: hand_out(pl.ds(48, 16)))
        return 0

    lax.fori_loop(0, BRICK, project, 0)

    wait_bytes(meta.at[pl.ds(1, RAY - 1)], recv_sem.at[1])
    own_first = (ray * 32).astype(F32)
    for b in range(4):
        row_keys.append(own_first + (b * 8 + row).astype(F32))
    row_keys = jnp.concatenate(row_keys, axis=0)
    columns = []
    for q in range(RAY // 2):
        key = jnp.where(
            lane < 64, meta[2 * q, 32:48, :].astype(F32)[0:8], meta[2 * q + 1, 32:48, :].astype(F32)[0:8]
        ) * 4.0 + (lane % 4).astype(F32)
        columns.append(jnp.where(row_keys == jnp.concatenate([key] * 12, axis=0), 1.0, 0.0))
    select = jnp.concatenate(columns, axis=1).astype(BF)
    sino_columns = []
    for q in range(4):
        owner = ((ray_x + q) % 4) * 4 + (ray_y + lane // 32) % 4
        key = (owner * 32 + lane % 32).astype(F32)
        sino_columns.append(jnp.where(row_keys[0:64] == jnp.concatenate([key] * 8, axis=0), 1.0, 0.0))
    sino_picked = jnp.dot(
        jnp.concatenate(sino_columns, axis=1).astype(BF), meta[:, 0:32, :].reshape(512, 128),
        preferred_element_type=F32,
    )
    select_own[...] = select[64:96]

    wait_bytes(contrib.at[pl.ds(1, RAY - 1)], recv_sem.at[3])
    picked[...] = (
        jnp.dot(select[0:64], contrib[...].reshape(1024, 128), preferred_element_type=F32) - sino_picked
    )

    above = (brick + BRICK - 1) % BRICK
    above_ray = (ray + (brick + BRICK - 1) // BRICK + RAY - 1) % RAY
    below = (brick + 1) % BRICK
    below_ray = (ray + (brick + 1) // BRICK) % RAY
    remote(
        est.at[:, pl.ds(56, 8), :], est_edges.at[0], send_sem.at[2], recv_sem.at[2], below_ray, below
    ).start()
    remote(
        est.at[:, pl.ds(0, 8), :], est_edges.at[1], send_sem.at[2], recv_sem.at[2], above_ray, above
    ).start()

    def split_left(m):
        mine = picked[pl.ds(pl.multiple_of(m * 8, 8), 8), :]
        return jnp.concatenate(
            [jnp.where(row < 4, mine, 0.0), jnp.where(row < 4, 0.0, mine)], axis=1
        ).astype(BF)

    def send_far():
        for edge, (last, column) in enumerate(((BRICK - 1, 15), (0, 0))):
            dz = (last // 2 + 4 - z) % 4
            dc = (last + core) % 2
            odd = dz % 2
            m = odd * (2 + dz // 2 + 2 * dc) + (1 - odd) * (3 * dz + dc)
            rim = jnp.dot(
                split_left(m),
                weights[m, :, :, column * 256 : column * 256 + 256].reshape(256, 256),
                preferred_element_type=F32,
            )
            far_out[edge] = jnp.concatenate([rim[:, :128], rim[:, 128:]], axis=0).astype(BF)
            remote(
                far_out.at[edge], far_in.at[brick], send_sem.at[7], recv_sem.at[7],
                (ray + (1, RAY - 1)[edge]) % RAY, (0, BRICK - 1)[edge],
            ).start()

    def backproject(t, _):
        pass_on = (t == 0) | (t == 1) | (t == 3) | (t == 6)
        g = jnp.where(pass_on, (t + 1) // 2, jnp.where(t == 5, 2, (t - 1) // 2))
        dz, first, stride = ring_step(g)
        dc = jnp.where(pass_on, 1, 0)
        m = first + dc * stride
        spread = jnp.dot(split_left(m), weights[m].reshape(256, 4096), preferred_element_type=F32)
        pieces = [
            jnp.concatenate(
                [spread[:, c * 256 : c * 256 + 128], spread[:, c * 256 + 128 : c * 256 + 256]], axis=0
            )
            for c in range(16)
        ]

        @pl.when(pass_on)
        def _():
            for c in range(16):
                mate_out[g, c] = pieces[c].astype(BF)
            remote(mate_out.at[g], mate_in.at[g], send_sem.at[4], mate_recv.at[g], ray, mate).start()
            pl.when(t == 1)(send_far)

        @pl.when(jnp.logical_not(pass_on))
        def _():
            wait_bytes(mate_in.at[g], mate_recv.at[g])
            for c in range(16):
                grad_out[g, c] = (pieces[c] + mate_in[g, c].astype(F32)).astype(BF)
            target = ((z + dz) % 4) * 2 + core

            @pl.when(g < 3)
            def _():
                remote(grad_out.at[g], grad_in.at[g], send_sem.at[5], recv_sem.at[5], ray, target).start()

            @pl.when(target < BRICK - 1)
            def _():
                remote(
                    grad_out.at[g, 15], halo_top.at[z], send_sem.at[6], recv_sem.at[6], ray, target + 1
                ).start()

            @pl.when(target > 0)
            def _():
                remote(
                    grad_out.at[g, 0], halo_low.at[z], send_sem.at[6], recv_sem.at[8], ray, target - 1
                ).start()

        return 0

    lax.fori_loop(0, BRICK, backproject, 0)

    res_ref[...] = (
        jnp.dot(select_own[...], contrib[...].reshape(1024, 128), preferred_element_type=F32) - sino[...]
    )

    wait_bytes(est_edges, recv_sem.at[2])
    wait_bytes(grad_in, recv_sem.at[5])
    total = grad_out[3].astype(F32)
    for g in range(3):
        total += grad_in[g].astype(F32)
    gathered[16:272, :] = total.reshape(256, 128)

    @pl.when(brick > 0)
    def _():
        wait_bytes(halo_top, recv_sem.at[6])
        gathered[0:16, :] = halo_top[...].astype(F32).sum(axis=0)

    @pl.when(brick < BRICK - 1)
    def _():
        wait_bytes(halo_low, recv_sem.at[8])
        gathered[272:288, :] = halo_low[...].astype(F32).sum(axis=0)

    @pl.when(brick == 0)
    def _():
        wait_bytes(far_in, recv_sem.at[7])
        gathered[0:16, :] = far_in[...].astype(F32).sum(axis=0)

    @pl.when(brick == BRICK - 1)
    def _():
        wait_bytes(far_in, recv_sem.at[7])
        gathered[272:288, :] = far_in[...].astype(F32).sum(axis=0)

    lane36 = lax.broadcasted_iota(jnp.int32, (36, 128), 1)
    for s in range(4):
        one = gathered[pl.ds(s, 36, stride=8), :]
        two = gathered[pl.ds(4 + s, 36, stride=8), :]
        anchor[s, pl.ds(0, 36, stride=2), :] = jnp.where(lane36 < 64, one, pltpu.roll(two, 64, 1))
        anchor[s, pl.ds(1, 36, stride=2), :] = jnp.where(lane36 < 64, pltpu.roll(one, 64, 1), two)
    image = jnp.concatenate([est_edges[0, :, 4:8, :], est[...], est_edges[1, :, 0:4, :]], axis=1)
    start = image - step_size * anchor[...]

    out_ref[...] = start

    wait_bytes(tiles.at[pl.ds(1, BRICK - 1)], send_sem.at[0])
    wait_bytes(meta.at[pl.ds(1, RAY - 1)], send_sem.at[1])
    wait_bytes(est_edges, send_sem.at[2])
    wait_bytes(contrib.at[pl.ds(1, RAY - 1)], send_sem.at[3])
    wait_bytes(mate_in, send_sem.at[4])
    wait_bytes(grad_in, send_sem.at[5])
    wait_bytes(tiles.at[0, pl.ds(0, 7)], send_sem.at[6])
    wait_bytes(far_out, send_sem.at[7])


def sweeps_kernel(start_ref, res_ref, out_hbm, res_hbm, out, save_sem):
    ray = lax.axis_index("ray")
    brick = lax.axis_index("brick")
    save_res = pltpu.make_async_copy(res_ref, res_hbm, save_sem.at[0])
    save_out = pltpu.make_async_copy(out, out_hbm, save_sem.at[1])
    save_res.start()

    shape = (4, 72, 128)
    rows = lax.broadcasted_iota(jnp.int32, shape, 1)
    lanes = lax.broadcasted_iota(jnp.int32, shape, 2)
    at_start = (ray == 0) & (brick == 0)
    at_end = (ray == RAY - 1) & (brick == BRICK - 1)
    above_image = (rows < 4) & at_start
    below_image = (rows >= 68) & at_end
    last_lane = lanes == 127
    first_lane = lanes == 0
    level = jnp.zeros((1, 72, 128), F32)

    start = jnp.where(below_image, 0.0, start_ref[...])
    primal = start
    extra = start
    dual_y = dual_x = dual_z = None
    for sweep in range(SWEEPS):
        diff_y = pltpu.roll(extra, 71, 1) - extra
        diff_x = jnp.where(last_lane, 0.0, pltpu.roll(extra, 127, 2)) - extra
        diff_z = jnp.concatenate([extra[1:] - extra[:-1], level], axis=0)
        trial_y, trial_x, trial_z = tv_step * diff_y, tv_step * diff_x, tv_step * diff_z
        if sweep:
            trial_y, trial_x, trial_z = dual_y + trial_y, dual_x + trial_x, dual_z + trial_z
        norm = trial_y * trial_y + trial_x * trial_x + trial_z * trial_z
        shrink = lax.rsqrt(jnp.maximum(1.0, norm * (1.0 / (tv_weight * tv_weight))))
        dual_y = jnp.where(above_image, 0.0, trial_y * shrink)
        dual_x = trial_x * shrink
        dual_z = trial_z * shrink
        div = dual_y - pltpu.roll(dual_y, 1, 1)
        div += dual_x - jnp.where(first_lane, 0.0, pltpu.roll(dual_x, 1, 2))
        div += dual_z - jnp.concatenate([level, dual_z[:-1]], axis=0)
        updated = (primal + tv_step * div + tv_step * start) * (1.0 / (1.0 + tv_step))
        extra = jnp.where(below_image, 0.0, 2.0 * updated - primal)
        primal = updated
    out[...] = primal[:, 4:68, :]
    save_out.start()
    save_res.wait()
    save_out.wait()


def shards(estimate, blocks, block_bundle, sinogram):
    dma = pltpu.SemaphoreType.DMA
    inputs = (estimate, blocks, block_bundle, sinogram.reshape(32, 128))
    start, residual = pl.pallas_call(
        kernel,
        out_shape=(
            jax.ShapeDtypeStruct((4, 72, 128), F32),
            jax.ShapeDtypeStruct((32, 128), F32),
        ),
        in_specs=[pl.BlockSpec(memory_space=pltpu.HBM)] * 4,
        out_specs=(pl.BlockSpec(memory_space=pltpu.VMEM), pl.BlockSpec(memory_space=pltpu.VMEM)),
        scratch_shapes=[
            pltpu.SMEM((1, 16), jnp.int32),
            pltpu.VMEM((4, 64, 128), F32),
            pltpu.VMEM((32, 128), F32),
            pltpu.VMEM((BRICK, 16, 16, 128), BF),
            pltpu.VMEM((256, 128), F32),
            pltpu.VMEM((BRICK, 2, 128, 4096), BF),
            pltpu.VMEM((RAY, 48, 128), BF),
            pltpu.VMEM((RAY, 64, 128), BF),
            pltpu.VMEM((64, 128), F32),
            pltpu.VMEM((32, 1024), BF),
            pltpu.VMEM((4, 16, 16, 128), BF),
            pltpu.VMEM((4, 16, 16, 128), BF),
            pltpu.VMEM((4, 16, 16, 128), BF),
            pltpu.VMEM((3, 16, 16, 128), BF),
            pltpu.VMEM((4, 16, 128), BF),
            pltpu.VMEM((4, 16, 128), BF),
            pltpu.VMEM((2, 16, 128), BF),
            pltpu.VMEM((BRICK, 16, 128), BF),
            pltpu.VMEM((2, 4, 8, 128), F32),
            pltpu.VMEM((288, 128), F32),
            pltpu.VMEM((4, 72, 128), F32),
            pltpu.SemaphoreType.REGULAR,
            dma((3,)),
            dma((BRICK,)),
            dma((BRICK,)),
            dma((4,)),
            dma((8,)),
            dma((9,)),
        ],
        compiler_params=pltpu.CompilerParams(
            collective_id=0, has_side_effects=True, vmem_limit_bytes=48 * 1024 * 1024
        ),
    )(*(pltpu.with_memory_space_constraint(array, pltpu.HBM) for array in inputs))
    restored, residual = pl.pallas_call(
        sweeps_kernel,
        out_shape=(
            jax.ShapeDtypeStruct((4, 64, 128), F32),
            jax.ShapeDtypeStruct((32, 128), F32),
        ),
        in_specs=[pl.BlockSpec(memory_space=pltpu.VMEM)] * 2,
        out_specs=(pl.BlockSpec(memory_space=pltpu.HBM),) * 2,
        scratch_shapes=[pltpu.VMEM((4, 64, 128), F32), dma((2,))],
        compiler_params=pltpu.CompilerParams(vmem_limit_bytes=16 * 1024 * 1024),
    )(start, residual)
    return restored, residual.reshape(sinogram.shape)


def solution(mesh):
    return jax.shard_map(
        shards,
        mesh=mesh,
        in_specs=(
            P(None, ("ray", "brick"), None),
            P("brick", "ray", None, None),
            P("brick", "ray"),
            P("brick", "ray", None, None),
        ),
        out_specs=(P(None, ("ray", "brick"), None), P("brick", "ray", None, None)),
        check_vma=False,
    )
```

```python
import jax
import jax.numpy as jnp
from jax import lax
from jax.experimental import pallas as pl
from jax.experimental.pallas import tpu as pltpu
from jax.sharding import PartitionSpec as P

RAY = 16
BRICK = 8
SWEEPS = 3
MESH = pl.DeviceIdType.MESH
BF = jnp.bfloat16
F32 = jnp.float32

step_size = 0.5
tv_step = 0.28
tv_weight = 0.5


def slot_offsets(m):
    third = (m + 2) // 4
    middle, last = third % 2, third // 2
    return (
        middle * (1 + 2 * (m % 2)) + 2 * last,
        middle * (m // 4) + (1 - middle) * (m % 2),
    )


RAY_STEPS = sorted(
    ((dx, dy) for dx in range(4) for dy in range(4) if dx or dy),
    key=lambda step: -(min(step[0], 4 - step[0]) + min(step[1], 4 - step[1])),
)


def ring_step(g):
    middle = ((g + 1) // 2) % 2
    step = (2 + g + (g // 2) * (1 - 2 * (g % 2))) % 4
    return step, middle * (4 - g) + (1 - middle) * (6 - 2 * g), 1 + middle


def kernel(
    est_hbm, blocks_hbm, bundle_hbm, sino_hbm,
    out_ref, res_ref,
    bundles, est, sino, tiles, tmp, weights, meta, contrib, picked, select_own, mate_out, mate_in, grad_out, grad_in,
    halo_top, halo_low, far_out, far_in, est_edges, gathered, anchor,
    line_sem, load_sem, weight_sem, tile_recv, mate_recv, send_sem, recv_sem,
):
    ray = lax.axis_index("ray")
    brick = lax.axis_index("brick")
    z, core = brick // 2, brick % 2
    mate = 2 * z + 1 - core
    ray_x, ray_y = ray // 4, ray % 4

    def ray_peer(dx, dy):
        return ((ray_x + dx) % 4) * 4 + (ray_y + dy) % 4

    def ray_slot(dx, dy):
        return ((4 - dx) % 4) * 4 + (4 - dy) % 4

    def tile_row(m):
        dz, dc = slot_offsets(m)
        return ((z + dz) % 4) * 2 + (core + dc) % 2

    def remote(src, dst, send, recv, to_ray, to_brick):
        return pltpu.make_async_remote_copy(
            src_ref=src, dst_ref=dst, send_sem=send, recv_sem=recv,
            device_id={"ray": to_ray, "brick": to_brick}, device_id_type=MESH,
        )

    def wait_bytes(ref, sem):
        pltpu.make_async_copy(ref, ref, sem).wait()

    load_est = pltpu.make_async_copy(est_hbm, est, load_sem.at[0])
    load_sino = pltpu.make_async_copy(sino_hbm, sino, load_sem.at[1])
    load_bundle = pltpu.make_async_copy(bundle_hbm, bundles, load_sem.at[2])
    load_est.start()

    barrier = pltpu.get_barrier_semaphore()

    def greet(to_ray, to_brick):
        pl.semaphore_signal(barrier, inc=1, device_id={"ray": to_ray, "brick": to_brick}, device_id_type=MESH)

    greet(ray, mate)
    for d in range(1, 4):
        greet(ray, (brick + 2 * d) % BRICK)
    for d in range(1, 4):
        greet(ray_peer(d, 0), brick)
        greet(ray_peer(0, d), brick)

    load_sino.start()
    load_bundle.start()


    lane = lax.broadcasted_iota(jnp.int32, (8, 128), 1)
    row = lax.broadcasted_iota(jnp.int32, (8, 128), 0)
    lane32 = lax.broadcasted_iota(jnp.int32, (32, 128), 1)

    load_est.wait()
    for s in range(4):
        even = est[s, pl.ds(0, 32, stride=2), :]
        odd = est[s, pl.ds(1, 32, stride=2), :]
        tmp[pl.ds(s, 32, stride=8), :] = jnp.where(lane32 < 64, even, pltpu.roll(odd, 64, 1))
        tmp[pl.ds(4 + s, 32, stride=8), :] = jnp.where(lane32 < 64, pltpu.roll(even, 64, 1), odd)
    tiles[0] = tmp[...].astype(BF).reshape(16, 16, 128)

    pl.semaphore_wait(barrier, 4 + 6)

    remote(tiles.at[0], tiles.at[1], send_sem.at[0], tile_recv.at[1], ray, mate).start()
    for step, slot in ((1, 2), (3, 3), (2, 6)):
        to = ((z + 4 - step) % 4) * 2 + core
        remote(tiles.at[0], tiles.at[slot], send_sem.at[0], tile_recv.at[slot], ray, to).start()

    def load_block(m, _):
        pltpu.make_async_copy(
            blocks_hbm.at[0, pl.ds(2 * tile_row(m), 2)], weights.at[m], weight_sem.at[m]
        ).start()
        return 0

    lax.fori_loop(0, BRICK, load_block, 0)

    for d in range(1, 4):
        pl.semaphore_signal(
            line_sem, inc=1, device_id={"ray": ray_peer(d, 0), "brick": brick}, device_id_type=MESH
        )

    load_bundle.wait()
    row_keys = []
    lane_key = jnp.zeros((8, 128), F32)
    for m in range(BRICK):
        first = bundles[0, 2 * tile_row(m)].astype(F32)
        second = bundles[0, 2 * tile_row(m) + 1].astype(F32)
        both = jnp.where(row < 4, first, second)
        row_keys.append(both * 4.0 + (row % 4).astype(F32))
        lane_key = jnp.where((lane % 64) // 8 == m, jnp.where((lane // 4) % 2 == 0, first, second), lane_key)
    load_sino.wait()
    meta[0, 0:32, :] = sino[...].astype(BF)
    meta[0, 32:48, :] = jnp.concatenate([lane_key, lane_key], axis=0).astype(BF)
    def send_meta():
        pl.semaphore_wait(line_sem, 3)
        for dx, dy in RAY_STEPS:
            remote(
                meta.at[0], meta.at[ray_slot(dx, dy)], send_sem.at[1], recv_sem.at[1], ray_peer(dx, dy), brick
            ).start()

    def project(m, _):
        @pl.when(m > 0)
        def _():
            wait_bytes(tiles.at[m], tile_recv.at[m])

        @pl.when((m == 2) | (m == 3) | (m == 6))
        def _():
            slot = m + 2 - m // 6
            remote(tiles.at[m], tiles.at[slot], send_sem.at[0], tile_recv.at[slot], ray, mate).start()

        wait_bytes(weights.at[m], weight_sem.at[m])
        held = tiles[m].astype(F32)
        left = jnp.concatenate(
            [half for c in range(16) for half in (held[c, 0:8], held[c, 8:16])], axis=1
        ).astype(BF)
        full = lax.dot_general(
            left, weights[m].reshape(256, 4096), (((1,), (1,)), ((), ())), preferred_element_type=F32
        )
        picked[pl.ds(pl.multiple_of(m * 8, 8), 8), :] = jnp.where(row < 4, full[:, :128], full[:, 128:])

        def hand_out(at):
            contrib[0, at, :] = picked[at, :].astype(BF)
            for dx, dy in RAY_STEPS:
                remote(
                    contrib.at[0, at], contrib.at[ray_slot(dx, dy), at], send_sem.at[3], recv_sem.at[3],
                    ray_peer(dx, dy), brick,
                ).start()

        pl.when(m == 1)(send_meta)
        pl.when(m == 5)(lambda: hand_out(pl.ds(0, 48)))
        pl.when(m == 7)(lambda: hand_out(pl.ds(48, 16)))
        return 0

    lax.fori_loop(0, BRICK, project, 0)

    wait_bytes(meta.at[pl.ds(1, RAY - 1)], recv_sem.at[1])
    own_first = (ray * 32).astype(F32)
    for b in range(4):
        row_keys.append(own_first + (b * 8 + row).astype(F32))
    row_keys = jnp.concatenate(row_keys, axis=0)
    columns = []
    for q in range(RAY // 2):
        key = jnp.where(
            lane < 64, meta[2 * q, 32:48, :].astype(F32)[0:8], meta[2 * q + 1, 32:48, :].astype(F32)[0:8]
        ) * 4.0 + (lane % 4).astype(F32)
        columns.append(jnp.where(row_keys == jnp.concatenate([key] * 12, axis=0), 1.0, 0.0))
    select = jnp.concatenate(columns, axis=1).astype(BF)
    sino_columns = []
    for q in range(4):
        owner = ((ray_x + q) % 4) * 4 + (ray_y + lane // 32) % 4
        key = (owner * 32 + lane % 32).astype(F32)
        sino_columns.append(jnp.where(row_keys[0:64] == jnp.concatenate([key] * 8, axis=0), 1.0, 0.0))
    sino_picked = jnp.dot(
        jnp.concatenate(sino_columns, axis=1).astype(BF), meta[:, 0:32, :].reshape(512, 128),
        preferred_element_type=F32,
    )
    select_own[...] = select[64:96]

    wait_bytes(contrib.at[pl.ds(1, RAY - 1)], recv_sem.at[3])
    picked[...] = (
        jnp.dot(select[0:64], contrib[...].reshape(1024, 128), preferred_element_type=F32) - sino_picked
    )

    above = (brick + BRICK - 1) % BRICK
    above_ray = (ray + (brick + BRICK - 1) // BRICK + RAY - 1) % RAY
    below = (brick + 1) % BRICK
    below_ray = (ray + (brick + 1) // BRICK) % RAY
    remote(
        est.at[:, pl.ds(56, 8), :], est_edges.at[0], send_sem.at[2], recv_sem.at[2], below_ray, below
    ).start()
    remote(
        est.at[:, pl.ds(0, 8), :], est_edges.at[1], send_sem.at[2], recv_sem.at[2], above_ray, above
    ).start()

    def split_left(m):
        mine = picked[pl.ds(pl.multiple_of(m * 8, 8), 8), :]
        return jnp.concatenate(
            [jnp.where(row < 4, mine, 0.0), jnp.where(row < 4, 0.0, mine)], axis=1
        ).astype(BF)

    def send_far():
        for edge, (last, column) in enumerate(((BRICK - 1, 15), (0, 0))):
            dz = (last // 2 + 4 - z) % 4
            dc = (last + core) % 2
            odd = dz % 2
            m = odd * (2 + dz // 2 + 2 * dc) + (1 - odd) * (3 * dz + dc)
            rim = jnp.dot(
                split_left(m),
                weights[m, :, :, column * 256 : column * 256 + 256].reshape(256, 256),
                preferred_element_type=F32,
            )
            far_out[edge] = jnp.concatenate([rim[:, :128], rim[:, 128:]], axis=0).astype(BF)
            remote(
                far_out.at[edge], far_in.at[brick], send_sem.at[7], recv_sem.at[7],
                (ray + (1, RAY - 1)[edge]) % RAY, (0, BRICK - 1)[edge],
            ).start()

    def backproject(t, _):
        pass_on = (t == 0) | (t == 1) | (t == 3) | (t == 6)
        g = jnp.where(pass_on, (t + 1) // 2, jnp.where(t == 5, 2, (t - 1) // 2))
        dz, first, stride = ring_step(g)
        dc = jnp.where(pass_on, 1, 0)
        m = first + dc * stride
        spread = jnp.dot(split_left(m), weights[m].reshape(256, 4096), preferred_element_type=F32)
        pieces = [
            jnp.concatenate(
                [spread[:, c * 256 : c * 256 + 128], spread[:, c * 256 + 128 : c * 256 + 256]], axis=0
            )
            for c in range(16)
        ]

        @pl.when(pass_on)
        def _():
            for c in range(16):
                mate_out[g, c] = pieces[c].astype(BF)
            remote(mate_out.at[g], mate_in.at[g], send_sem.at[4], mate_recv.at[g], ray, mate).start()
            pl.when(t == 1)(send_far)

        @pl.when(jnp.logical_not(pass_on))
        def _():
            wait_bytes(mate_in.at[g], mate_recv.at[g])
            for c in range(16):
                grad_out[g, c] = (pieces[c] + mate_in[g, c].astype(F32)).astype(BF)
            target = ((z + dz) % 4) * 2 + core

            @pl.when(g < 3)
            def _():
                remote(grad_out.at[g], grad_in.at[g], send_sem.at[5], recv_sem.at[5], ray, target).start()

            @pl.when(target < BRICK - 1)
            def _():
                remote(
                    grad_out.at[g, 15], halo_top.at[z], send_sem.at[6], recv_sem.at[6], ray, target + 1
                ).start()

            @pl.when(target > 0)
            def _():
                remote(
                    grad_out.at[g, 0], halo_low.at[z], send_sem.at[6], recv_sem.at[8], ray, target - 1
                ).start()

        return 0

    lax.fori_loop(0, BRICK, backproject, 0)

    res_ref[...] = (
        jnp.dot(select_own[...], contrib[...].reshape(1024, 128), preferred_element_type=F32) - sino[...]
    )

    wait_bytes(est_edges, recv_sem.at[2])
    wait_bytes(grad_in, recv_sem.at[5])
    total = grad_out[3].astype(F32)
    for g in range(3):
        total += grad_in[g].astype(F32)
    gathered[16:272, :] = total.reshape(256, 128)

    @pl.when(brick > 0)
    def _():
        wait_bytes(halo_top, recv_sem.at[6])
        gathered[0:16, :] = halo_top[...].astype(F32).sum(axis=0)

    @pl.when(brick < BRICK - 1)
    def _():
        wait_bytes(halo_low, recv_sem.at[8])
        gathered[272:288, :] = halo_low[...].astype(F32).sum(axis=0)

    @pl.when(brick == 0)
    def _():
        wait_bytes(far_in, recv_sem.at[7])
        gathered[0:16, :] = far_in[...].astype(F32).sum(axis=0)

    @pl.when(brick == BRICK - 1)
    def _():
        wait_bytes(far_in, recv_sem.at[7])
        gathered[272:288, :] = far_in[...].astype(F32).sum(axis=0)

    lane36 = lax.broadcasted_iota(jnp.int32, (36, 128), 1)
    for s in range(4):
        one = gathered[pl.ds(s, 36, stride=8), :]
        two = gathered[pl.ds(4 + s, 36, stride=8), :]
        anchor[s, pl.ds(0, 36, stride=2), :] = jnp.where(lane36 < 64, one, pltpu.roll(two, 64, 1))
        anchor[s, pl.ds(1, 36, stride=2), :] = jnp.where(lane36 < 64, pltpu.roll(one, 64, 1), two)
    image = jnp.concatenate([est_edges[0, :, 4:8, :], est[...], est_edges[1, :, 0:4, :]], axis=1)
    start = image - step_size * anchor[...]

    out_ref[...] = start

    wait_bytes(tiles.at[pl.ds(1, BRICK - 1)], send_sem.at[0])
    wait_bytes(meta.at[pl.ds(1, RAY - 1)], send_sem.at[1])
    wait_bytes(est_edges, send_sem.at[2])
    wait_bytes(contrib.at[pl.ds(1, RAY - 1)], send_sem.at[3])
    wait_bytes(mate_in, send_sem.at[4])
    wait_bytes(grad_in, send_sem.at[5])
    wait_bytes(tiles.at[0, pl.ds(0, 7)], send_sem.at[6])
    wait_bytes(far_out, send_sem.at[7])


def sweeps_kernel(start_ref, res_ref, out_hbm, res_hbm, out, save_sem):
    ray = lax.axis_index("ray")
    brick = lax.axis_index("brick")
    save_res = pltpu.make_async_copy(res_ref, res_hbm, save_sem.at[0])
    save_out = pltpu.make_async_copy(out, out_hbm, save_sem.at[1])
    save_res.start()

    shape = (4, 72, 128)
    rows = lax.broadcasted_iota(jnp.int32, shape, 1)
    lanes = lax.broadcasted_iota(jnp.int32, shape, 2)
    at_start = (ray == 0) & (brick == 0)
    at_end = (ray == RAY - 1) & (brick == BRICK - 1)
    above_image = (rows < 4) & at_start
    below_image = (rows >= 68) & at_end
    last_lane = lanes == 127
    first_lane = lanes == 0
    level = jnp.zeros((1, 72, 128), F32)

    start = jnp.where(below_image, 0.0, start_ref[...])
    primal = start
    extra = start
    dual_y = dual_x = dual_z = None
    for sweep in range(SWEEPS):
        diff_y = pltpu.roll(extra, 71, 1) - extra
        diff_x = jnp.where(last_lane, 0.0, pltpu.roll(extra, 127, 2)) - extra
        diff_z = jnp.concatenate([extra[1:] - extra[:-1], level], axis=0)
        trial_y, trial_x, trial_z = tv_step * diff_y, tv_step * diff_x, tv_step * diff_z
        if sweep:
            trial_y, trial_x, trial_z = dual_y + trial_y, dual_x + trial_x, dual_z + trial_z
        norm = trial_y * trial_y + trial_x * trial_x + trial_z * trial_z
        shrink = lax.rsqrt(jnp.maximum(1.0, norm * (1.0 / (tv_weight * tv_weight))))
        dual_y = jnp.where(above_image, 0.0, trial_y * shrink)
        dual_x = trial_x * shrink
        dual_z = trial_z * shrink
        div = dual_y - pltpu.roll(dual_y, 1, 1)
        div += dual_x - jnp.where(first_lane, 0.0, pltpu.roll(dual_x, 1, 2))
        div += dual_z - jnp.concatenate([level, dual_z[:-1]], axis=0)
        updated = (primal + tv_step * div + tv_step * start) * (1.0 / (1.0 + tv_step))
        extra = jnp.where(below_image, 0.0, 2.0 * updated - primal)
        primal = updated
    out[...] = primal[:, 4:68, :]
    save_out.start()
    save_res.wait()
    save_out.wait()


def shards(estimate, blocks, block_bundle, sinogram):
    dma = pltpu.SemaphoreType.DMA
    inputs = (estimate, blocks, block_bundle, sinogram.reshape(32, 128))
    start, residual = pl.pallas_call(
        kernel,
        out_shape=(
            jax.ShapeDtypeStruct((4, 72, 128), F32),
            jax.ShapeDtypeStruct((32, 128), F32),
        ),
        in_specs=[pl.BlockSpec(memory_space=pltpu.HBM)] * 4,
        out_specs=(pl.BlockSpec(memory_space=pltpu.VMEM), pl.BlockSpec(memory_space=pltpu.VMEM)),
        scratch_shapes=[
            pltpu.SMEM((1, 16), jnp.int32),
            pltpu.VMEM((4, 64, 128), F32),
            pltpu.VMEM((32, 128), F32),
            pltpu.VMEM((BRICK, 16, 16, 128), BF),
            pltpu.VMEM((256, 128), F32),
            pltpu.VMEM((BRICK, 2, 128, 4096), BF),
            pltpu.VMEM((RAY, 48, 128), BF),
            pltpu.VMEM((RAY, 64, 128), BF),
            pltpu.VMEM((64, 128), F32),
            pltpu.VMEM((32, 1024), BF),
            pltpu.VMEM((4, 16, 16, 128), BF),
            pltpu.VMEM((4, 16, 16, 128), BF),
            pltpu.VMEM((4, 16, 16, 128), BF),
            pltpu.VMEM((3, 16, 16, 128), BF),
            pltpu.VMEM((4, 16, 128), BF),
            pltpu.VMEM((4, 16, 128), BF),
            pltpu.VMEM((2, 16, 128), BF),
            pltpu.VMEM((BRICK, 16, 128), BF),
            pltpu.VMEM((2, 4, 8, 128), F32),
            pltpu.VMEM((288, 128), F32),
            pltpu.VMEM((4, 72, 128), F32),
            pltpu.SemaphoreType.REGULAR,
            dma((3,)),
            dma((BRICK,)),
            dma((BRICK,)),
            dma((4,)),
            dma((8,)),
            dma((9,)),
        ],
        compiler_params=pltpu.CompilerParams(
            collective_id=0, has_side_effects=True, vmem_limit_bytes=48 * 1024 * 1024
        ),
    )(*(pltpu.with_memory_space_constraint(array, pltpu.HBM) for array in inputs))
    restored, residual = pl.pallas_call(
        sweeps_kernel,
        out_shape=(
            jax.ShapeDtypeStruct((4, 64, 128), F32),
            jax.ShapeDtypeStruct((32, 128), F32),
        ),
        in_specs=[pl.BlockSpec(memory_space=pltpu.VMEM)] * 2,
        out_specs=(pl.BlockSpec(memory_space=pltpu.HBM),) * 2,
        scratch_shapes=[pltpu.VMEM((4, 64, 128), F32), dma((2,))],
        compiler_params=pltpu.CompilerParams(vmem_limit_bytes=16 * 1024 * 1024),
    )(start, residual)
    return restored, residual.reshape(sinogram.shape)


def solution(mesh):
    return jax.shard_map(
        shards,
        mesh=mesh,
        in_specs=(
            P(None, ("ray", "brick"), None),
            P("brick", "ray", None, None),
            P("brick", "ray"),
            P("brick", "ray", None, None),
        ),
        out_specs=(P(None, ("ray", "brick"), None), P("brick", "ray", None, None)),
        check_vma=False,
    )
```
